256 devices in a mesh: row: 8 (over z), col: 32 (over y, x, core).
Axes of the slice: x: 4, y: 4, z: 8, core: 2. Of those that a mesh axis runs over, the one named last changes fastest.
Arguments:
- acts: bfloat16 [2048, 8192], P('col', 'row'), may hold values from -6 to 6
- out_grads: bfloat16 [2048, 28672], P('row', 'col'), may hold values from -0.19921875 to 0.19921875
- weight: bfloat16 [8192, 28672], P('row', 'col'), may hold values from -0.0625 to 0.0625
- momentum: float32 [8192, 28672], P('row', 'col'), may hold values from -40 to 40, as said below
- basis: float32 [28672, 256], P('col'), may hold values from -0.03125 to 0.03125
Outputs:
- new_weight: bfloat16 [8192, 28672], P('row', 'col')
- new_momentum: float32 [8192, 28672], P('row', 'col')
- new_basis: float32 [28672, 256], P('col')
The draws below stay inside these ranges and needn't reach their ends.
Inputs may be any that keep to these rules, and one draw needn't show every extreme that they name: momentum is a float32 matrix.
All inputs are finite; a program needn't handle non-finite values.
Results may differ from the reference program's by a relative error of at most 0.00065.
Values may be sent and summed in bfloat16 or wider, within the bound.
No kernel may reach another device: no remote copies, remote signals or barrier semaphores. Data moves between devices by JAX's collectives and lax.ppermute only.
A program may use at most 64 MiB of HBM per device.

```python
import math
import jax
import jax.numpy as jnp
from jax import lax

D = 8192
FF = 28672
RANK = 256
TOKENS = 2048


def draw_momentum(key, part):
    key = jax.random.fold_in(key, 7)
    first = jax.random.fold_in(key, 0)
    third = jax.random.fold_in(key, 2)
    base = jax.random.normal(first, (D, FF), jnp.float32)
    col_scale = jnp.exp(jax.random.uniform(third, (1, FF), jnp.float32, -0.6, 0.6))
    value = base * col_scale
    return jnp.clip(value, -40.0, 40.0)


def block_scale(own_key, dims, cuts, low, high):
    level, own = 1.0, jax.random.fold_in(own_key, 6)
    for position, blocks in cuts:
        heights = jnp.exp(jax.random.uniform(jax.random.fold_in(own, position), (blocks,), jnp.float32, low / len(cuts), high / len(cuts)))
        level = level * jnp.repeat(heights, dims[position] // blocks).reshape([-1 if axis == position else 1 for axis in range(len(dims))])
    return level


def noise(key, shape, spread, most, pieces=(), dtype=jnp.bfloat16):
    drawn = spread * jax.random.normal(key, shape, jnp.float32)
    if pieces:
        drawn = drawn * block_scale(key, shape, pieces, -0.22, 0.18)
    return jnp.clip(drawn, -most, most).astype(dtype)


def setup_inputs(seed: int = 0) -> dict:
    splits = jax.random.split(jax.random.key(seed), 6)
    acts = noise(splits[0], (TOKENS, D), 1.0, 6.0, ((0, 32), (1, 8)))
    out_grads = noise(splits[1], (TOKENS, FF), 0.03125, 0.19921875, ((0, 8), (1, 32)))
    weight = noise(splits[2], (D, FF), D ** -0.5, 0.0625, ((0, 8), (1, 32)))
    momentum = draw_momentum(jax.random.fold_in(splits[5], 71), 0)
    basis = noise(splits[4], (FF, RANK), FF ** -0.5, 0.03125, ((0, 32),), jnp.float32)
    return dict(acts=acts, out_grads=out_grads, weight=weight, momentum=momentum, basis=basis)


keep_rate = 0.95
step_rate = 0.01
norm_eps = 1e-06

def reference(acts, out_grads, weight, momentum, basis):
    highest = lax.Precision.HIGHEST
    grad = jnp.dot(acts.T.astype(jnp.float32), out_grads.astype(jnp.float32), preferred_element_type=jnp.float32)
    buffer = momentum + grad
    proj = jnp.dot(buffer, basis, precision=highest)
    gram = jnp.dot(proj.T, proj, precision=highest)
    lower = jnp.linalg.cholesky(gram)
    ortho = jax.scipy.linalg.solve_triangular(lower, proj.T, lower=True).T
    back = jnp.dot(buffer.T, ortho, precision=highest)
    norms = lax.optimization_barrier(jnp.sum(back * back, axis=0))
    new_momentum = buffer - (1.0 - keep_rate) * jnp.dot(ortho, back.T, precision=highest)
    new_basis = back / jnp.sqrt(norms + norm_eps)
    factor = step_rate * math.sqrt(D * FF / RANK)
    new_weight = (weight.astype(jnp.float32) - factor * jnp.dot(ortho, new_basis.T, precision=highest)).astype(jnp.bfloat16)
    return (new_weight, new_momentum, new_basis)
```

```python
import math

import jax
import jax.numpy as jnp
from jax import lax
from jax.experimental import pallas as pl
from jax.experimental.pallas import tpu as pltpu
from jax.sharding import PartitionSpec as P

D = 8192
FF = 28672
RANK = 256

keep_rate = 0.95
step_rate = 0.01
norm_eps = 1e-06

ROWS = 8
COLS = 32
CHIPS = 16
VMEM_LIMIT = 48 * 1024 * 1024
BLOCK = 32
STEP = 16

UP = [(i, (i + 1) % ROWS) for i in range(ROWS)]
DOWN = [(i, (i - 1) % ROWS) for i in range(ROWS)]
CORE_SWAP = [(i, i ^ 1) for i in range(COLS)]
SAME_CORE = [[2 * i + k for i in range(CHIPS)] for k in range(2)]


def split(x):
    high = x.astype(jnp.bfloat16)
    low = (x - high.astype(jnp.float32)).astype(jnp.bfloat16)
    return high, low


def dot3(a, b, dims):
    a_high, a_low = split(a)
    b_high, b_low = split(b)

    def mul(x, y):
        return lax.dot_general(x, y, (dims, ((), ())), preferred_element_type=jnp.float32)

    return mul(a_high, b_high) + (mul(a_high, b_low) + mul(a_low, b_high))


def spread(x, axis, size, groups=None):
    copies = jnp.broadcast_to(x[None], (size,) + x.shape)
    return lax.all_to_all(copies, axis, 0, 0, axis_index_groups=groups)


def whole(x):
    return pl.BlockSpec(x.shape, lambda *_: (0,) * len(x.shape))


def across(height, width):
    return pl.BlockSpec((height, width), lambda i, *_: (i, 0))


def proj_kernel(place, acts, *refs):
    weights, (local, proj) = refs[:-2], refs[-2:]
    rank = proj.shape[1]
    total = local[...]
    for n, w in enumerate(weights):
        tokens = w.shape[0]
        start = pl.multiple_of(place[n] * tokens, tokens)
        high, low = split(w[...])
        both = lax.dot_general(
            acts[pl.ds(start, tokens), :],
            jnp.concatenate([high, low], axis=1),
            (((0,), (0,)), ((), ())),
            preferred_element_type=jnp.float32,
        )
        total += both[:, :rank] + both[:, rank:]
    proj[...] = total


def proj_part(place, acts, weights, local):
    tokens, rows = acts.shape
    rank = local.shape[1]
    tile = 256
    return pl.pallas_call(
        proj_kernel,
        grid_spec=pltpu.PrefetchScalarGridSpec(
            num_scalar_prefetch=1,
            grid=(rows // tile,),
            in_specs=[pl.BlockSpec((tokens, tile), lambda i, _: (0, i))]
            + [whole(w) for w in weights]
            + [across(tile, rank)],
            out_specs=across(tile, rank),
        ),
        out_shape=jax.ShapeDtypeStruct((rows, rank), jnp.float32),
        compiler_params=pltpu.CompilerParams(vmem_limit_bytes=VMEM_LIMIT),
        cost_estimate=pl.CostEstimate(
            flops=4 * tokens * rows * rank, bytes_accessed=2 * tokens * rows + 16 * rows * rank, transcendentals=0
        ),
        name="proj_part",
    )(place, acts, *weights, local)


def grad_kernel(place, acts, *refs):
    pieces, (momentum, buffer) = refs[:-2], refs[-2:]
    total = momentum[...]
    for n, g in enumerate(pieces):
        tokens = g.shape[0]
        start = pl.multiple_of(place[n] * tokens, tokens)
        total += lax.dot_general(
            acts[pl.ds(start, tokens), :],
            g[...],
            (((0,), (0,)), ((), ())),
            preferred_element_type=jnp.float32,
        )
    buffer[...] = total


def add_grad(place, acts, pieces, momentum):
    rows, cols = momentum.shape
    tokens = acts.shape[0]
    tile = 256
    return pl.pallas_call(
        grad_kernel,
        grid_spec=pltpu.PrefetchScalarGridSpec(
            num_scalar_prefetch=1,
            grid=(rows // tile,),
            in_specs=[pl.BlockSpec((tokens, tile), lambda i, _: (0, i))]
            + [whole(g) for g in pieces]
            + [across(tile, cols)],
            out_specs=across(tile, cols),
        ),
        out_shape=jax.ShapeDtypeStruct((rows, cols), jnp.float32),
        compiler_params=pltpu.CompilerParams(vmem_limit_bytes=VMEM_LIMIT),
        cost_estimate=pl.CostEstimate(
            flops=2 * tokens * rows * cols,
            bytes_accessed=2 * tokens * (rows + cols) + 8 * rows * cols,
            transcendentals=0,
        ),
        name="add_grad",
    )(place, acts, *pieces, momentum)


def factor_kernel(gram, inverse, work):
    n = gram.shape[0]
    lanes = 128
    repeat = n // lanes
    work[...] = gram[...]
    rows = lax.broadcasted_iota(jnp.int32, (BLOCK, lanes), 0)
    row = lax.broadcasted_iota(jnp.int32, (BLOCK, n), 0)
    lane = lax.broadcasted_iota(jnp.int32, (BLOCK, n), 1)
    for first in range(0, n, BLOCK):
        last = first + BLOCK
        part = work[first:last, :]
        pivots = jnp.ones((BLOCK, lanes), jnp.float32)
        for j in range(0, BLOCK, STEP):
            at = first + j
            cols = [jnp.broadcast_to(part[:, at + k : at + k + 1], (BLOCK, lanes)) for k in range(STEP)]
            unit = jnp.where(lane - first == row, 1.0, 0.0)
            part = jnp.where((lane >= at) & (lane < at + STEP), unit, part)
            ratios = []
            for k in range(STEP):
                here = j + k
                pivot = cols[k][here : here + 1, :]
                pivots = jnp.where(rows == here, pivot, pivots)
                ratio = jnp.where(rows > here, cols[k] * (1.0 / pivot), 0.0)
                ratios.append(ratio)
                for m in range(k + 1, STEP):
                    cols[m] = cols[m] - ratio * cols[m][here : here + 1, :]
            for k in range(STEP):
                here = j + k
                part = part - jnp.concatenate([ratios[k]] * repeat, axis=1) * part[here : here + 1, :]
        part = part * jnp.concatenate([lax.rsqrt(pivots)] * repeat, axis=1)
        inverse[first:last, :] = jnp.where(lane < last, part, 0.0)
        if last < n:
            rest = work[last:, :]
            lane_rest = lax.broadcasted_iota(jnp.int32, rest.shape, 1)
            rest = jnp.where((lane_rest >= first) & (lane_rest < last), 0.0, rest)
            work[last:, :] = rest - lax.dot_general(
                part[:, last:],
                part,
                (((0,), (0,)), ((), ())),
                precision=lax.Precision.HIGHEST,
                preferred_element_type=jnp.float32,
            )


def inverse_factor(gram):
    n = gram.shape[0]
    return pl.pallas_call(
        factor_kernel,
        out_shape=jax.ShapeDtypeStruct((n, n), jnp.float32),
        scratch_shapes=[pltpu.VMEM((n, n), jnp.float32)],
        cost_estimate=pl.CostEstimate(flops=10**10, bytes_accessed=8 * n * n, transcendentals=0),
        name="inverse_factor",
    )(gram)


def update_kernel(buffer, weight, ortho, cross, inverse, scale, new_momentum, new_weight, new_basis, back):
    factor = step_rate * math.sqrt(D * FF / RANK)
    last = ((1,), (1,))

    @pl.when(pl.program_id(0) == 0)
    def _():
        height = back.shape[0] // cross.shape[0]
        for n in range(cross.shape[0]):
            span = slice(n * height, (n + 1) * height)
            back[span, :] = dot3(cross[n, :height, :], inverse[...], last)
        new_basis[...] = back[...] * scale[...]

    left = ortho[...]
    right = back[...]
    fix = lax.dot_general(
        left.astype(jnp.bfloat16),
        right.astype(jnp.bfloat16),
        (last, ((), ())),
        preferred_element_type=jnp.float32,
    )
    new_momentum[...] = buffer[...] - (1.0 - keep_rate) * fix
    step = dot3(left * scale[...], right, last)
    new_weight[...] = (weight[...].astype(jnp.float32) - factor * step).astype(jnp.bfloat16)


def update(buffer, weight, ortho, cross, inverse, scale):
    rows, cols = buffer.shape
    rank = ortho.shape[1]
    tile = 256
    return pl.pallas_call(
        update_kernel,
        grid=(rows // tile,),
        in_specs=[
            across(tile, cols),
            across(tile, cols),
            across(tile, rank),
            whole(cross),
            whole(inverse),
            whole(scale),
        ],
        out_specs=[across(tile, cols), across(tile, cols), pl.BlockSpec((cols, rank), lambda i: (0, 0))],
        out_shape=[
            jax.ShapeDtypeStruct((rows, cols), jnp.float32),
            jax.ShapeDtypeStruct((rows, cols), jnp.bfloat16),
            jax.ShapeDtypeStruct((cols, rank), jnp.float32),
        ],
        scratch_shapes=[pltpu.VMEM((cols, rank), jnp.float32)],
        compiler_params=pltpu.CompilerParams(vmem_limit_bytes=VMEM_LIMIT),
        name="update",
    )(buffer, weight, ortho, cross, inverse, scale)


def in_order(core, mine, other, axis):
    first = core == 0
    return jnp.stack([jnp.where(first, mine, other), jnp.where(first, other, mine)], axis=axis)


def on_device(acts, out_grads, weight, momentum, basis):
    high = lax.Precision.HIGH
    highest = lax.Precision.HIGHEST
    row = lax.axis_index("row")
    col = lax.axis_index("col")
    core = col % 2
    rank = basis.shape[1]

    with jax.named_scope("gather_acts"):
        acts_all = lax.all_gather(acts, "col", axis=0, tiled=True)

    with jax.named_scope("gather_grads"):
        pieces, places = [out_grads], [row]
        up = down = out_grads
        for step in range(1, ROWS // 2):
            up = lax.ppermute(up, "row", UP)
            down = lax.ppermute(down, "row", DOWN)
            pieces += [up, down]
            places += [row - step, row + step]
        cut = out_grads.shape[0] // 2
        far_up = lax.ppermute(up[:cut], "row", UP)
        far_down = lax.ppermute(down[cut:], "row", DOWN)
        pieces.append(jnp.concatenate([far_up, far_down], axis=0))
        places.append(row + ROWS // 2)
        place = jnp.stack(places).astype(jnp.int32) % ROWS

    with jax.named_scope("proj"):
        local = jnp.dot(momentum, basis, precision=high)
        weights = [jnp.dot(g.astype(jnp.float32), basis, precision=high) for g in pieces]
        part = proj_part(place, acts_all, weights, local)

    with jax.named_scope("sum_proj"):
        cut = part.shape[0] // 2
        halves = part.reshape(2, cut, rank)
        away = lax.dynamic_index_in_dim(halves, 1 - core, 0, keepdims=False)
        mine = lax.dynamic_index_in_dim(halves, core, 0, keepdims=False)
        mine = mine + lax.ppermute(away, "col", CORE_SWAP)
        shares = mine.reshape(CHIPS, cut // CHIPS, rank)
        shares = lax.all_to_all(shares, "col", 0, 0, axis_index_groups=SAME_CORE)
        buffer = add_grad(place, acts_all, pieces, momentum)
        shares, buffer = lax.optimization_barrier((shares, buffer))
        mine = spread(jnp.sum(shares, axis=0), "col", CHIPS, SAME_CORE).reshape(cut, rank)
        other = lax.ppermute(mine, "col", CORE_SWAP)
        proj = in_order(core, mine, other, 0).reshape(2 * cut, rank)

    with jax.named_scope("cross"):
        cross = lax.dot_general(buffer, proj, (((0,), (0,)), ((), ())), precision=high)
        share = lax.psum_scatter(cross, "row", scatter_dimension=0, tiled=True)

    with jax.named_scope("gram"):
        width = rank // COLS
        slab = lax.dynamic_slice_in_dim(proj, col * width, width, axis=1)
        gram = lax.dot_general(slab, proj, (((0,), (0,)), ((), ())), precision=highest)
        gram = jnp.sum(spread(gram, "row", ROWS), axis=0)
        gram = spread(gram, "col", COLS).reshape(rank, rank)

    inverse = inverse_factor(gram)
    share, inverse = lax.optimization_barrier((share, inverse))
    ortho = lax.dot_general(proj, inverse, (((1,), (1,)), ((), ())), precision=highest)

    with jax.named_scope("gather_cross"):
        filled = jnp.pad(share, ((0, 128 - share.shape[0]), (0, 0)))
        cross_all = lax.all_gather(filled, "row", axis=0)

    with jax.named_scope("norms"):
        back = lax.dot_general(share, inverse, (((1,), (1,)), ((), ())), precision=highest)
        norms = jnp.sum(back * back, axis=0, keepdims=True)
        norms = jnp.sum(spread(norms, ("row", "col"), ROWS * COLS), axis=0)
        scale = 1.0 / jnp.sqrt(norms + norm_eps)

    new_momentum, new_weight, new_basis = update(buffer, weight, ortho, cross_all, inverse, scale)
    return (new_weight, new_momentum, new_basis)


def solution(mesh):
    return jax.shard_map(
        on_device,
        mesh=mesh,
        in_specs=(
            P("col", "row"),
            P("row", "col"),
            P("row", "col"),
            P("row", "col"),
            P("col", None),
        ),
        out_specs=(P("row", "col"), P("row", "col"), P("col", None)),
        check_vma=False,
    )
```

```python
import math

import jax
import jax.numpy as jnp
from jax import lax
from jax.experimental import pallas as pl
from jax.experimental.pallas import tpu as pltpu
from jax.sharding import PartitionSpec as P

D = 8192
FF = 28672
RANK = 256

keep_rate = 0.95
step_rate = 0.01
norm_eps = 1e-06

ROWS = 8
COLS = 32
CHIPS = 16
VMEM_LIMIT = 48 * 1024 * 1024
BLOCK = 32
STEP = 16

UP = [(i, (i + 1) % ROWS) for i in range(ROWS)]
DOWN = [(i, (i - 1) % ROWS) for i in range(ROWS)]
CORE_SWAP = [(i, i ^ 1) for i in range(COLS)]
SAME_CORE = [[2 * i + k for i in range(CHIPS)] for k in range(2)]
GROUPS = COLS // ROWS
MIXERS = [[GROUPS * i + k for i in range(ROWS)] for k in range(GROUPS)]


def split(x):
    high = x.astype(jnp.bfloat16)
    low = (x - high.astype(jnp.float32)).astype(jnp.bfloat16)
    return high, low


def dot3(a, b, dims):
    a_high, a_low = split(a)
    b_high, b_low = split(b)

    def mul(x, y):
        return lax.dot_general(x, y, (dims, ((), ())), preferred_element_type=jnp.float32)

    return mul(a_high, b_high) + (mul(a_high, b_low) + mul(a_low, b_high))


def spread(x, axis, size, groups=None):
    copies = jnp.broadcast_to(x[None], (size,) + x.shape)
    return lax.all_to_all(copies, axis, 0, 0, axis_index_groups=groups)


def whole(x):
    return pl.BlockSpec(x.shape, lambda *_: (0,) * len(x.shape))


def across(height, width):
    return pl.BlockSpec((height, width), lambda i, *_: (i, 0))


def grad_kernel(place, acts, *refs):
    pieces, (momentum, buffer) = refs[:-2], refs[-2:]
    total = momentum[...]
    for n, g in enumerate(pieces):
        tokens = g.shape[0]
        start = pl.multiple_of(place[n] * tokens, tokens)
        total += lax.dot_general(
            acts[pl.ds(start, tokens), :],
            g[...],
            (((0,), (0,)), ((), ())),
            preferred_element_type=jnp.float32,
        )
    buffer[...] = total


def add_grad(place, acts, pieces, momentum):
    rows, cols = momentum.shape
    tokens = acts.shape[0]
    tile = 256
    return pl.pallas_call(
        grad_kernel,
        grid_spec=pltpu.PrefetchScalarGridSpec(
            num_scalar_prefetch=1,
            grid=(rows // tile,),
            in_specs=[pl.BlockSpec((tokens, tile), lambda i, _: (0, i))]
            + [whole(g) for g in pieces]
            + [across(tile, cols)],
            out_specs=across(tile, cols),
        ),
        out_shape=jax.ShapeDtypeStruct((rows, cols), jnp.float32),
        compiler_params=pltpu.CompilerParams(vmem_limit_bytes=VMEM_LIMIT),
        cost_estimate=pl.CostEstimate(
            flops=2 * tokens * rows * cols,
            bytes_accessed=2 * tokens * (rows + cols) + 8 * rows * cols,
            transcendentals=0,
        ),
        name="add_grad",
    )(place, acts, *pieces, momentum)


def factor_kernel(gram, inverse, work):
    n = gram.shape[0]
    lanes = 128
    repeat = n // lanes
    work[...] = gram[...]
    rows = lax.broadcasted_iota(jnp.int32, (BLOCK, lanes), 0)
    row = lax.broadcasted_iota(jnp.int32, (BLOCK, n), 0)
    lane = lax.broadcasted_iota(jnp.int32, (BLOCK, n), 1)
    for first in range(0, n, BLOCK):
        last = first + BLOCK
        part = work[first:last, :]
        pivots = jnp.ones((BLOCK, lanes), jnp.float32)
        for j in range(0, BLOCK, STEP):
            at = first + j
            cols = [jnp.broadcast_to(part[:, at + k : at + k + 1], (BLOCK, lanes)) for k in range(STEP)]
            unit = jnp.where(lane - first == row, 1.0, 0.0)
            part = jnp.where((lane >= at) & (lane < at + STEP), unit, part)
            ratios = []
            for k in range(STEP):
                here = j + k
                pivot = cols[k][here : here + 1, :]
                pivots = jnp.where(rows == here, pivot, pivots)
                ratio = jnp.where(rows > here, cols[k] * (1.0 / pivot), 0.0)
                ratios.append(ratio)
                for m in range(k + 1, STEP):
                    cols[m] = cols[m] - ratio * cols[m][here : here + 1, :]
            for k in range(STEP):
                here = j + k
                part = part - jnp.concatenate([ratios[k]] * repeat, axis=1) * part[here : here + 1, :]
        part = part * jnp.concatenate([lax.rsqrt(pivots)] * repeat, axis=1)
        inverse[first:last, :] = jnp.where(lane < last, part, 0.0)
        if last < n:
            rest = work[last:, :]
            lane_rest = lax.broadcasted_iota(jnp.int32, rest.shape, 1)
            rest = jnp.where((lane_rest >= first) & (lane_rest < last), 0.0, rest)
            work[last:, :] = rest - lax.dot_general(
                part[:, last:],
                part,
                (((0,), (0,)), ((), ())),
                precision=lax.Precision.HIGHEST,
                preferred_element_type=jnp.float32,
            )


def inverse_factor(gram):
    n = gram.shape[0]
    return pl.pallas_call(
        factor_kernel,
        out_shape=jax.ShapeDtypeStruct((n, n), jnp.float32),
        scratch_shapes=[pltpu.VMEM((n, n), jnp.float32)],
        cost_estimate=pl.CostEstimate(flops=10**10, bytes_accessed=8 * n * n, transcendentals=0),
        name="inverse_factor",
    )(gram)


def update_kernel(buffer, weight, ortho, cross, inverse, scale, new_momentum, new_weight, new_basis, back):
    factor = step_rate * math.sqrt(D * FF / RANK)
    last = ((1,), (1,))

    @pl.when(pl.program_id(0) == 0)
    def _():
        height = back.shape[0] // cross.shape[0]
        for n in range(cross.shape[0]):
            span = slice(n * height, (n + 1) * height)
            back[span, :] = dot3(cross[n, :height, :], inverse[...], last)
        new_basis[...] = back[...] * scale[...]

    left = ortho[...]
    right = back[...]
    fix = lax.dot_general(
        left.astype(jnp.bfloat16),
        right.astype(jnp.bfloat16),
        (last, ((), ())),
        preferred_element_type=jnp.float32,
    )
    new_momentum[...] = buffer[...] - (1.0 - keep_rate) * fix
    step = dot3(left * scale[...], right, last)
    new_weight[...] = (weight[...].astype(jnp.float32) - factor * step).astype(jnp.bfloat16)


def update(buffer, weight, ortho, cross, inverse, scale):
    rows, cols = buffer.shape
    rank = ortho.shape[1]
    tile = 256
    return pl.pallas_call(
        update_kernel,
        grid=(rows // tile,),
        in_specs=[
            across(tile, cols),
            across(tile, cols),
            across(tile, rank),
            whole(cross),
            whole(inverse),
            whole(scale),
        ],
        out_specs=[across(tile, cols), across(tile, cols), pl.BlockSpec((cols, rank), lambda i: (0, 0))],
        out_shape=[
            jax.ShapeDtypeStruct((rows, cols), jnp.float32),
            jax.ShapeDtypeStruct((rows, cols), jnp.bfloat16),
            jax.ShapeDtypeStruct((cols, rank), jnp.float32),
        ],
        scratch_shapes=[pltpu.VMEM((cols, rank), jnp.float32)],
        compiler_params=pltpu.CompilerParams(vmem_limit_bytes=VMEM_LIMIT),
        name="update",
    )(buffer, weight, ortho, cross, inverse, scale)


def in_order(core, mine, other, axis):
    first = core == 0
    return jnp.stack([jnp.where(first, mine, other), jnp.where(first, other, mine)], axis=axis)


def on_device(acts, out_grads, weight, momentum, basis):
    high = lax.Precision.HIGH
    highest = lax.Precision.HIGHEST
    row = lax.axis_index("row")
    col = lax.axis_index("col")
    core = col % 2
    rank = basis.shape[1]

    with jax.named_scope("gather_acts"):
        acts_all = lax.all_gather(acts, "col", axis=0, tiled=True)

    pieces, places = [out_grads], [row]
    up = down = out_grads

    def turn(step, *others):
        nonlocal up, down
        with jax.named_scope("gather_grads"):
            up = lax.ppermute(up, "row", UP)
            down = lax.ppermute(down, "row", DOWN)
            pieces.extend([up, down])
            places.extend([row - step, row + step])
            up, down, *others = lax.optimization_barrier((up, down, *others))
            return others

    with jax.named_scope("proj"):
        small = jnp.dot(out_grads.astype(jnp.float32), basis, precision=high)
        small = small.reshape(GROUPS, ROWS, -1, rank).swapaxes(0, 1).reshape(COLS, -1, rank)
        small = jnp.sum(lax.all_to_all(small, "col", 0, 0), axis=0)
        mixed = acts.reshape(ROWS, -1, acts.shape[1])
        small, mixed = turn(1, small, mixed)
        mixed = lax.all_to_all(mixed, "col", 0, 0, axis_index_groups=MIXERS)
        small, mixed = turn(2, small, mixed)
        local = jnp.dot(momentum, basis, precision=high)
        small = spread(small, "row", ROWS).reshape(-1, rank)
        mixed = mixed.reshape(-1, acts.shape[1]).astype(jnp.float32)
        part = local + lax.dot_general(mixed, small, (((0,), (0,)), ((), ())), precision=high)
        (part,) = turn(3, part)

    with jax.named_scope("gather_grads"):
        cut = out_grads.shape[0] // 2
        far_up = lax.ppermute(up[:cut], "row", UP)
        far_down = lax.ppermute(down[cut:], "row", DOWN)
        pieces.append(jnp.concatenate([far_up, far_down], axis=0))
        places.append(row + ROWS // 2)
        place = jnp.stack(places).astype(jnp.int32) % ROWS

    with jax.named_scope("sum_proj"):
        cut = part.shape[0] // 2
        halves = part.reshape(2, cut, rank)
        away = lax.dynamic_index_in_dim(halves, 1 - core, 0, keepdims=False)
        mine = lax.dynamic_index_in_dim(halves, core, 0, keepdims=False)
        mine = mine + lax.ppermute(away, "col", CORE_SWAP)
        shares = mine.reshape(CHIPS, cut // CHIPS, rank)
        shares = lax.all_to_all(shares, "col", 0, 0, axis_index_groups=SAME_CORE)
        buffer = add_grad(place, acts_all, pieces, momentum)
        shares, buffer = lax.optimization_barrier((shares, buffer))
        mine = spread(jnp.sum(shares, axis=0), "col", CHIPS, SAME_CORE).reshape(cut, rank)
        other = lax.ppermute(mine, "col", CORE_SWAP)
        proj = in_order(core, mine, other, 0).reshape(2 * cut, rank)

    with jax.named_scope("cross"):
        cross = lax.dot_general(buffer, proj, (((0,), (0,)), ((), ())), precision=high)
        share = lax.psum_scatter(cross, "row", scatter_dimension=0, tiled=True)

    with jax.named_scope("gram"):
        width = rank // COLS
        slab = lax.dynamic_slice_in_dim(proj, col * width, width, axis=1)
        gram = lax.dot_general(slab, proj, (((0,), (0,)), ((), ())), precision=highest)
        gram = jnp.sum(spread(gram, "row", ROWS), axis=0)
        gram = spread(gram, "col", COLS).reshape(rank, rank)

    inverse = inverse_factor(gram)
    share, inverse = lax.optimization_barrier((share, inverse))
    ortho = lax.dot_general(proj, inverse, (((1,), (1,)), ((), ())), precision=highest)

    with jax.named_scope("gather_cross"):
        filled = jnp.pad(share, ((0, 128 - share.shape[0]), (0, 0)))
        cross_all = lax.all_gather(filled, "row", axis=0)

    with jax.named_scope("norms"):
        back = lax.dot_general(share, inverse, (((1,), (1,)), ((), ())), precision=highest)
        norms = jnp.sum(back * back, axis=0, keepdims=True)
        norms = jnp.sum(spread(norms, ("row", "col"), ROWS * COLS), axis=0)
        scale = 1.0 / jnp.sqrt(norms + norm_eps)

    new_momentum, new_weight, new_basis = update(buffer, weight, ortho, cross_all, inverse, scale)
    return (new_weight, new_momentum, new_basis)


def solution(mesh):
    return jax.shard_map(
        on_device,
        mesh=mesh,
        in_specs=(
            P("col", "row"),
            P("row", "col"),
            P("row", "col"),
            P("row", "col"),
            P("col", None),
        ),
        out_specs=(P("row", "col"), P("row", "col"), P("col", None)),
        check_vma=False,
    )
```

```python
import math

import jax
import jax.numpy as jnp
from jax import lax
from jax.experimental import pallas as pl
from jax.experimental.pallas import tpu as pltpu
from jax.sharding import PartitionSpec as P

D = 8192
FF = 28672
RANK = 256

keep_rate = 0.95
step_rate = 0.01
norm_eps = 1e-06

ROWS = 8
COLS = 32
CHIPS = 16
VMEM_LIMIT = 24 * 1024 * 1024
VMEM_MOST = 60 * 1024 * 1024
BLOCK = 64
STEP = 16
TILES = 4

UP = [(i, (i + 1) % ROWS) for i in range(ROWS)]
DOWN = [(i, (i - 1) % ROWS) for i in range(ROWS)]
CORE_SWAP = [(i, i ^ 1) for i in range(COLS)]
SAME_CORE = [[2 * i + k for i in range(CHIPS)] for k in range(2)]
GROUPS = COLS // ROWS
MIXERS = [[GROUPS * i + k for i in range(ROWS)] for k in range(GROUPS)]


def split(x):
    high = x.astype(jnp.bfloat16)
    low = (x - high.astype(jnp.float32)).astype(jnp.bfloat16)
    return high, low


def dot3(a, b, dims):
    a_high, a_low = split(a)
    b_high, b_low = split(b)

    def mul(x, y):
        return lax.dot_general(x, y, (dims, ((), ())), preferred_element_type=jnp.float32)

    return mul(a_high, b_high) + (mul(a_high, b_low) + mul(a_low, b_high))


def spread(x, axis, size, groups=None):
    copies = jnp.broadcast_to(x[None], (size,) + x.shape)
    return lax.all_to_all(copies, axis, 0, 0, axis_index_groups=groups)


def in_vmem():
    return pl.BlockSpec(memory_space=pltpu.VMEM)


def grad_kernel(place, acts, *refs):
    pieces, (momentum, buffer, left, right, total, sems) = refs[:-6], refs[-6:]
    tokens = right.shape[0] // len(pieces)
    rows = total.shape[0]
    tile = rows // TILES
    fetches = []
    for n, g in enumerate(pieces):
        span = pl.ds(pl.multiple_of(place[n] * tokens, tokens), tokens)
        fetches.append(pltpu.make_async_copy(g, right.at[span, :], sems.at[n]))
    spans = [pl.ds(n * tile, tile) for n in range(TILES)]
    lefts = [pltpu.make_async_copy(acts.at[:, at], left.at[n], sems.at[len(pieces) + n]) for n, at in enumerate(spans)]
    olds = [
        pltpu.make_async_copy(momentum.at[at, :], total.at[at, :], sems.at[len(pieces) + TILES + n])
        for n, at in enumerate(spans)
    ]
    news = [
        pltpu.make_async_copy(total.at[at, :], buffer.at[at, :], sems.at[len(pieces) + 2 * TILES + n])
        for n, at in enumerate(spans)
    ]
    lefts[0].start()
    for copy in fetches:
        copy.start()
    olds[0].start()
    for n in range(1, TILES):
        lefts[n].start()
        olds[n].start()
    for copy in fetches:
        copy.wait()
    for n in range(TILES):
        lefts[n].wait()
        grad = lax.dot_general(
            left[n], right[...], (((0,), (0,)), ((), ())), preferred_element_type=jnp.float32
        )
        olds[n].wait()
        total[spans[n], :] += grad
        news[n].start()
    for copy in news:
        copy.wait()


def add_grad(place, acts, pieces, momentum):
    rows, cols = momentum.shape
    tokens = acts.shape[0]
    anywhere = pl.BlockSpec(memory_space=pl.ANY)
    return pl.pallas_call(
        grad_kernel,
        in_specs=[pl.BlockSpec(memory_space=pltpu.SMEM)] + [anywhere] * (len(pieces) + 2),
        out_specs=anywhere,
        out_shape=jax.ShapeDtypeStruct((rows, cols), jnp.float32),
        scratch_shapes=[
            pltpu.VMEM((TILES, tokens, rows // TILES), jnp.bfloat16),
            pltpu.VMEM((tokens, cols), jnp.bfloat16),
            pltpu.VMEM((rows, cols), jnp.float32),
            pltpu.SemaphoreType.DMA((len(pieces) + 3 * TILES,)),
        ],
        compiler_params=pltpu.CompilerParams(vmem_limit_bytes=VMEM_MOST),
        cost_estimate=pl.CostEstimate(
            flops=2 * tokens * rows * cols,
            bytes_accessed=2 * tokens * (rows + cols) + 8 * rows * cols,
            transcendentals=0,
        ),
        name="add_grad",
    )(place, acts, *pieces, momentum)


def cross_kernel(core, buffer, mine, other, cross, held, sems):
    cut = mine.shape[0]
    tile = held.shape[1]
    copies, sides = [], []
    for n in range(held.shape[0]):
        half, at = divmod(n * tile, cut)
        side = core[0] if half == 0 else 1 - core[0]
        start = pl.multiple_of(side * cut + at, tile)
        copies.append(pltpu.make_async_copy(buffer.at[pl.ds(start, tile), :], held.at[n], sems.at[n]))
        sides.append((mine, other)[half][at : at + tile, :])
    for copy in copies:
        copy.start()
    total = None
    for n, copy in enumerate(copies):
        copy.wait()
        term = dot3(held[n], sides[n], ((0,), (0,)))
        total = term if total is None else total + term
    cross[...] = total


def cross_part(core, buffer, mine, other):
    rows, cols = buffer.shape
    return pl.pallas_call(
        cross_kernel,
        in_specs=[pl.BlockSpec(memory_space=pltpu.SMEM), pl.BlockSpec(memory_space=pl.ANY)] + [in_vmem()] * 2,
        out_specs=in_vmem(),
        out_shape=jax.ShapeDtypeStruct((cols, mine.shape[1]), jnp.float32),
        scratch_shapes=[
            pltpu.VMEM((TILES, rows // TILES, cols), jnp.float32),
            pltpu.SemaphoreType.DMA((TILES,)),
        ],
        compiler_params=pltpu.CompilerParams(vmem_limit_bytes=VMEM_MOST),
        name="cross",
    )(core, buffer, mine, other)


def factor_kernel(gram, inverse, work):
    n = gram.shape[0]
    lanes = 128
    repeat = n // lanes
    work[...] = gram[...]
    rows = lax.broadcasted_iota(jnp.int32, (BLOCK, lanes), 0)
    row = lax.broadcasted_iota(jnp.int32, (BLOCK, n), 0)
    lane = lax.broadcasted_iota(jnp.int32, (BLOCK, n), 1)
    for first in range(0, n, BLOCK):
        last = first + BLOCK
        part = work[first:last, :]
        pivots = jnp.ones((BLOCK, lanes), jnp.float32)
        for j in range(0, BLOCK, STEP):
            at = first + j
            cols = [jnp.broadcast_to(part[:, at + k : at + k + 1], (BLOCK, lanes)) for k in range(STEP)]
            unit = jnp.where(lane - first == row, 1.0, 0.0)
            part = jnp.where((lane >= at) & (lane < at + STEP), unit, part)
            ratios = []
            for k in range(STEP):
                here = j + k
                pivot = cols[k][here : here + 1, :]
                pivots = jnp.where(rows == here, pivot, pivots)
                ratio = jnp.where(rows > here, cols[k] * (1.0 / pivot), 0.0)
                ratios.append(ratio)
                for m in range(k + 1, STEP):
                    cols[m] = cols[m] - ratio * cols[m][here : here + 1, :]
            for k in range(STEP):
                here = j + k
                part = part - jnp.concatenate([ratios[k]] * repeat, axis=1) * part[here : here + 1, :]
        part = part * jnp.concatenate([lax.rsqrt(pivots)] * repeat, axis=1)
        inverse[first:last, :] = jnp.where(lane < last, part, 0.0)
        if last < n:
            rest = work[last:, :]
            lane_rest = lax.broadcasted_iota(jnp.int32, rest.shape, 1)
            rest = jnp.where((lane_rest >= first) & (lane_rest < last), 0.0, rest)
            work[last:, :] = rest - lax.dot_general(
                part[:, last:],
                part,
                (((0,), (0,)), ((), ())),
                precision=lax.Precision.HIGHEST,
                preferred_element_type=jnp.float32,
            )


def inverse_factor(gram):
    n = gram.shape[0]
    return pl.pallas_call(
        factor_kernel,
        out_shape=jax.ShapeDtypeStruct((n, n), jnp.float32),
        scratch_shapes=[pltpu.VMEM((n, n), jnp.float32)],
        cost_estimate=pl.CostEstimate(flops=10**10, bytes_accessed=8 * n * n, transcendentals=0),
        name="inverse_factor",
    )(gram)


def back_kernel(place, inverse, s0, s1, s2, s3, s4, s5, s6, s7, back, norms):
    for n, share in enumerate((s0, s1, s2, s3, s4, s5, s6, s7)):
        height = share.shape[0]
        start = pl.multiple_of(place[n] * height, height)
        back[pl.ds(start, height), :] = dot3(share[...], inverse[...], ((1,), (1,)))
    whole = back[...]
    norms[...] = jnp.sum(whole * whole, axis=0, keepdims=True)


def back_and_norms(place, inverse, shares):
    rank = inverse.shape[0]
    cols = len(shares) * shares[0].shape[0]
    return pl.pallas_call(
        back_kernel,
        in_specs=[pl.BlockSpec(memory_space=pltpu.SMEM)] + [in_vmem()] * (1 + len(shares)),
        out_specs=[in_vmem()] * 2,
        out_shape=[
            jax.ShapeDtypeStruct((cols, rank), jnp.float32),
            jax.ShapeDtypeStruct((1, rank), jnp.float32),
        ],
        compiler_params=pltpu.CompilerParams(vmem_limit_bytes=VMEM_LIMIT),
        name="back_and_norms",
    )(place, inverse, *shares)


def momentum_kernel(buffer, ortho, back, new_momentum):
    fix = lax.dot_general(
        ortho[...].astype(jnp.bfloat16),
        back[...].astype(jnp.bfloat16),
        (((1,), (1,)), ((), ())),
        preferred_element_type=jnp.float32,
    )
    new_momentum[...] = buffer[...] - (1.0 - keep_rate) * fix


def update_momentum(buffer, ortho, back):
    rows, cols = buffer.shape
    rank = ortho.shape[1]
    tile = rows // TILES
    part = lambda width: pl.BlockSpec((tile, width), lambda i: (i, 0))
    return pl.pallas_call(
        momentum_kernel,
        grid=(TILES,),
        in_specs=[part(cols), part(rank), pl.BlockSpec(back.shape, lambda i: (0, 0))],
        out_specs=part(cols),
        out_shape=jax.ShapeDtypeStruct((rows, cols), jnp.float32),
        compiler_params=pltpu.CompilerParams(vmem_limit_bytes=VMEM_LIMIT),
        name="update_momentum",
    )(buffer, ortho, back)


def weight_kernel(weight, ortho, back, scale, new_weight, new_basis, basis, stepped, sems):
    factor = step_rate * math.sqrt(D * FF / RANK)
    right = back[...]
    basis[...] = right * scale[...]
    stores = []

    def store(source, target):
        copy = pltpu.make_async_copy(source, target, sems.at[len(stores)])
        copy.start()
        stores.append(copy)

    store(basis, new_basis)
    tile = weight.shape[0] // TILES
    for n in range(TILES):
        span = slice(n * tile, (n + 1) * tile)
        step = dot3(ortho[span, :] * scale[...], right, ((1,), (1,)))
        stepped[span, :] = (weight[span, :].astype(jnp.float32) - factor * step).astype(jnp.bfloat16)
        store(stepped.at[span, :], new_weight.at[span, :])
    for copy in stores:
        copy.wait()


def update_weight(weight, ortho, back, scale):
    rows, cols = weight.shape
    rank = ortho.shape[1]
    return pl.pallas_call(
        weight_kernel,
        in_specs=[in_vmem()] * 4,
        out_specs=[pl.BlockSpec(memory_space=pl.ANY)] * 2,
        out_shape=[
            jax.ShapeDtypeStruct((rows, cols), jnp.bfloat16),
            jax.ShapeDtypeStruct((cols, rank), jnp.float32),
        ],
        scratch_shapes=[
            pltpu.VMEM((cols, rank), jnp.float32),
            pltpu.VMEM((rows, cols), jnp.bfloat16),
            pltpu.SemaphoreType.DMA((1 + TILES,)),
        ],
        compiler_params=pltpu.CompilerParams(vmem_limit_bytes=VMEM_LIMIT),
        name="update_weight",
    )(weight, ortho, back, scale)


def call(kernel, name, shape, *args, scalars=0):
    many = isinstance(shape, list)
    return pl.pallas_call(
        kernel,
        in_specs=[pl.BlockSpec(memory_space=pltpu.SMEM)] * scalars + [in_vmem()] * (len(args) - scalars),
        out_specs=[in_vmem()] * len(shape) if many else in_vmem(),
        out_shape=[jax.ShapeDtypeStruct(x, jnp.float32) for x in shape]
        if many
        else jax.ShapeDtypeStruct(shape, jnp.float32),
        compiler_params=pltpu.CompilerParams(vmem_limit_bytes=VMEM_LIMIT),
        name=name,
    )(*args)


def sum_kernel(shares, copies):
    total = shares[0]
    for n in range(1, shares.shape[0]):
        total = total + shares[n]
    for n in range(copies.shape[0]):
        copies[n] = total


def sum_copies(shares, count):
    return call(sum_kernel, "sum_copies", (count,) + shares.shape[1:], shares)


def pick_kernel(core, part, other, mine):
    cut = mine.shape[0]
    span = pl.ds(pl.multiple_of(core[0] * cut, cut), cut)
    mine[...] = part[span, :] + other[span, :]


def gram_kernel(col, mine, other, copies):
    gram = jnp.zeros((mine.shape[1], mine.shape[1]), jnp.float32)
    for half in (mine, other):
        gram = gram + lax.dot_general(
            half[...],
            half[...],
            (((0,), (0,)), ((), ())),
            precision=lax.Precision.HIGHEST,
            preferred_element_type=jnp.float32,
        )
    copies[0] = jnp.zeros(copies.shape[1:], jnp.float32)
    height = copies.shape[1]
    for n in range(COLS):

        @pl.when(col[0] == n)
        def _():
            for m in range(copies.shape[0]):
                copies[m] = gram[n * height : (n + 1) * height, :]


def part_kernel(local, mixed, small, part):
    high, low = split(small[...])
    rank = small.shape[1]
    both = lax.dot_general(
        mixed[...],
        jnp.concatenate([high, low], axis=1),
        (((0,), (0,)), ((), ())),
        preferred_element_type=jnp.float32,
    )
    part[...] = local[...] + (both[:, :rank] + both[:, rank:])


def proj_part(local, mixed, small):
    return pl.pallas_call(
        part_kernel,
        in_specs=[in_vmem()] * 3,
        out_specs=in_vmem(),
        out_shape=jax.ShapeDtypeStruct(local.shape, jnp.float32),
        compiler_params=pltpu.CompilerParams(vmem_limit_bytes=VMEM_LIMIT),
        name="proj_part",
    )(local, mixed, small)


def on_device(acts, out_grads, weight, momentum, basis):
    high = lax.Precision.HIGH
    highest = lax.Precision.HIGHEST
    row = lax.axis_index("row")
    col = lax.axis_index("col")
    core = (col % 2).reshape(1)
    rank = basis.shape[1]

    with jax.named_scope("gather_acts"):
        acts_all = lax.all_gather(acts, "col", axis=0, tiled=True)

    pieces, places = [out_grads], [row]
    up = down = out_grads

    def turn(step, *others):
        nonlocal up, down
        with jax.named_scope("gather_grads"):
            up = lax.ppermute(up, "row", UP)
            down = lax.ppermute(down, "row", DOWN)
            pieces.extend([up, down])
            places.extend([row - step, row + step])
            up, down, *others = lax.optimization_barrier((up, down, *others))
            return others

    with jax.named_scope("proj"):
        small = jnp.dot(out_grads.astype(jnp.float32), basis, precision=high)
        small = small.reshape(GROUPS, ROWS, -1, rank).swapaxes(0, 1).reshape(COLS, -1, rank)
        small = sum_copies(lax.all_to_all(small, "col", 0, 0), ROWS)
        mixed = acts.reshape(ROWS, -1, acts.shape[1])
        local = jnp.dot(momentum, basis, precision=high)
        small, mixed, local = turn(1, small, mixed, local)
        mixed = lax.all_to_all(mixed, "col", 0, 0, axis_index_groups=MIXERS)
        small, mixed = turn(2, small, mixed)
        small = lax.all_to_all(small, "row", 0, 0).reshape(-1, rank)
        part = proj_part(local, mixed.reshape(-1, acts.shape[1]), small)
        (part,) = turn(3, part)

    with jax.named_scope("gather_grads"):
        pieces.append(lax.ppermute(up, "row", UP))
        places.append(row + ROWS // 2)
        place = jnp.stack(places).astype(jnp.int32) % ROWS

    with jax.named_scope("sum_proj"):
        cut = part.shape[0] // 2
        other = lax.ppermute(part, "col", CORE_SWAP)
        mine = call(pick_kernel, "pick", (cut, rank), core, part, other, scalars=1)
        shares = mine.reshape(CHIPS, cut // CHIPS, rank)
        shares = lax.all_to_all(shares, "col", 0, 0, axis_index_groups=SAME_CORE)
        buffer = add_grad(place, acts_all, pieces, momentum)
        mine = sum_copies(shares, CHIPS)
        mine = lax.all_to_all(mine, "col", 0, 0, axis_index_groups=SAME_CORE).reshape(cut, rank)
        mine, buffer = lax.optimization_barrier((mine, buffer))
        other = lax.ppermute(mine, "col", CORE_SWAP)

    with jax.named_scope("cross"):
        cross = cross_part(core, buffer, mine, other)
        cross, mine, other = lax.optimization_barrier((cross, mine, other))
        share = lax.psum_scatter(cross, "row", scatter_dimension=0, tiled=True)

    with jax.named_scope("gram"):
        height = rank // COLS
        gram = call(gram_kernel, "gram", (ROWS, height, rank), col.reshape(1), mine, other, scalars=1)
        gram = sum_copies(lax.all_to_all(gram, "row", 0, 0), COLS)
        gram = lax.all_to_all(gram, "col", 0, 0).reshape(rank, rank)

    inverse = inverse_factor(gram)
    share, inverse = lax.optimization_barrier((share, inverse))
    first = core[0] == 0
    proj = jnp.concatenate([jnp.where(first, mine, other), jnp.where(first, other, mine)], axis=0)
    ortho = lax.dot_general(proj, inverse, (((1,), (1,)), ((), ())), precision=highest)

    with jax.named_scope("gather_cross"):
        parts = [share]
        up = down = share
        for _ in range(1, ROWS // 2):
            up = lax.ppermute(up, "row", UP)
            down = lax.ppermute(down, "row", DOWN)
            parts += [up, down]
        parts.append(lax.ppermute(up, "row", UP))

    back, norms = back_and_norms(place, inverse, parts)

    with jax.named_scope("norms"):
        norms = jnp.sum(spread(norms, "col", COLS), axis=0)
        scale = 1.0 / jnp.sqrt(norms + norm_eps)

    new_momentum = update_momentum(buffer, ortho, back)
    new_weight, new_basis = update_weight(weight, ortho, back, scale)
    return (new_weight, new_momentum, new_basis)


def solution(mesh):
    return jax.shard_map(
        on_device,
        mesh=mesh,
        in_specs=(
            P("col", "row"),
            P("row", "col"),
            P("row", "col"),
            P("row", "col"),
            P("col", None),
        ),
        out_specs=(P("row", "col"), P("row", "col"), P("col", None)),
        check_vma=False,
    )
```

```python
import math

import jax
import jax.numpy as jnp
from jax import lax
from jax.experimental import pallas as pl
from jax.experimental.pallas import tpu as pltpu
from jax.sharding import PartitionSpec as P

D = 8192
FF = 28672
RANK = 256

keep_rate = 0.95
step_rate = 0.01
norm_eps = 1e-06

ROWS = 8
COLS = 32
CHIPS = 16
VMEM_LIMIT = 24 * 1024 * 1024
VMEM_MOST = 60 * 1024 * 1024
BLOCK = 64
STEP = 16
TILES = 4

UP = [(i, (i + 1) % ROWS) for i in range(ROWS)]
DOWN = [(i, (i - 1) % ROWS) for i in range(ROWS)]
CORE_SWAP = [(i, i ^ 1) for i in range(COLS)]
SAME_CORE = [[2 * i + k for i in range(CHIPS)] for k in range(2)]
GROUPS = COLS // ROWS
MIXERS = [[GROUPS * i + k for i in range(ROWS)] for k in range(GROUPS)]


def split(x):
    high = x.astype(jnp.bfloat16)
    low = (x - high.astype(jnp.float32)).astype(jnp.bfloat16)
    return high, low


def dot3(a, b, dims):
    a_high, a_low = split(a)
    b_high, b_low = split(b)

    def mul(x, y):
        return lax.dot_general(x, y, (dims, ((), ())), preferred_element_type=jnp.float32)

    return mul(a_high, b_high) + (mul(a_high, b_low) + mul(a_low, b_high))


def spread(x, axis, size, groups=None):
    copies = jnp.broadcast_to(x[None], (size,) + x.shape)
    return lax.all_to_all(copies, axis, 0, 0, axis_index_groups=groups)


def in_vmem():
    return pl.BlockSpec(memory_space=pltpu.VMEM)


def grad_kernel(place, acts, *refs):
    pieces, (momentum, buffer, left, right, total, sems) = refs[:-6], refs[-6:]
    tokens = right.shape[0] // len(pieces)
    rows = total.shape[0]
    tile = rows // TILES
    fetches = []
    for n, g in enumerate(pieces):
        span = pl.ds(pl.multiple_of(place[n] * tokens, tokens), tokens)
        fetches.append(pltpu.make_async_copy(g, right.at[span, :], sems.at[n]))
    spans = [pl.ds(n * tile, tile) for n in range(TILES)]
    lefts = [pltpu.make_async_copy(acts.at[:, at], left.at[n], sems.at[len(pieces) + n]) for n, at in enumerate(spans)]
    olds = [
        pltpu.make_async_copy(momentum.at[at, :], total.at[at, :], sems.at[len(pieces) + TILES + n])
        for n, at in enumerate(spans)
    ]
    news = [
        pltpu.make_async_copy(total.at[at, :], buffer.at[at, :], sems.at[len(pieces) + 2 * TILES + n])
        for n, at in enumerate(spans)
    ]
    lefts[0].start()
    for copy in fetches:
        copy.start()
    olds[0].start()
    for n in range(1, TILES):
        lefts[n].start()
        olds[n].start()
    for copy in fetches:
        copy.wait()
    for n in range(TILES):
        lefts[n].wait()
        grad = lax.dot_general(
            left[n], right[...], (((0,), (0,)), ((), ())), preferred_element_type=jnp.float32
        )
        olds[n].wait()
        total[spans[n], :] += grad
        news[n].start()
    for copy in news:
        copy.wait()


def add_grad(place, acts, pieces, momentum):
    rows, cols = momentum.shape
    tokens = acts.shape[0]
    anywhere = pl.BlockSpec(memory_space=pl.ANY)
    return pl.pallas_call(
        grad_kernel,
        in_specs=[pl.BlockSpec(memory_space=pltpu.SMEM)] + [anywhere] * (len(pieces) + 2),
        out_specs=anywhere,
        out_shape=jax.ShapeDtypeStruct((rows, cols), jnp.float32),
        scratch_shapes=[
            pltpu.VMEM((TILES, tokens, rows // TILES), jnp.bfloat16),
            pltpu.VMEM((tokens, cols), jnp.bfloat16),
            pltpu.VMEM((rows, cols), jnp.float32),
            pltpu.SemaphoreType.DMA((len(pieces) + 3 * TILES,)),
        ],
        compiler_params=pltpu.CompilerParams(vmem_limit_bytes=VMEM_MOST),
        cost_estimate=pl.CostEstimate(
            flops=2 * tokens * rows * cols,
            bytes_accessed=2 * tokens * (rows + cols) + 8 * rows * cols,
            transcendentals=0,
        ),
        name="add_grad",
    )(place, acts, *pieces, momentum)


def cross_kernel(core, buffer, mine, other, cross):
    cut = mine.shape[0]
    here = pl.ds(pl.multiple_of(core[0] * cut, cut), cut)
    there = pl.ds(pl.multiple_of((1 - core[0]) * cut, cut), cut)
    first = ((0,), (0,))
    cross[...] = dot3(buffer[here, :], mine[...], first) + dot3(buffer[there, :], other[...], first)


def factor_kernel(gram, inverse, work):
    n = gram.shape[0]
    lanes = 128
    repeat = n // lanes
    work[...] = gram[...]
    rows = lax.broadcasted_iota(jnp.int32, (BLOCK, lanes), 0)
    row = lax.broadcasted_iota(jnp.int32, (BLOCK, n), 0)
    lane = lax.broadcasted_iota(jnp.int32, (BLOCK, n), 1)
    for first in range(0, n, BLOCK):
        last = first + BLOCK
        part = work[first:last, :]
        pivots = jnp.ones((BLOCK, lanes), jnp.float32)
        for j in range(0, BLOCK, STEP):
            at = first + j
            cols = [jnp.broadcast_to(part[:, at + k : at + k + 1], (BLOCK, lanes)) for k in range(STEP)]
            unit = jnp.where(lane - first == row, 1.0, 0.0)
            part = jnp.where((lane >= at) & (lane < at + STEP), unit, part)
            ratios = []
            for k in range(STEP):
                here = j + k
                pivot = cols[k][here : here + 1, :]
                pivots = jnp.where(rows == here, pivot, pivots)
                ratio = jnp.where(rows > here, cols[k] * (1.0 / pivot), 0.0)
                ratios.append(ratio)
                for m in range(k + 1, STEP):
                    cols[m] = cols[m] - ratio * cols[m][here : here + 1, :]
            for k in range(STEP):
                here = j + k
                part = part - jnp.concatenate([ratios[k]] * repeat, axis=1) * part[here : here + 1, :]
        part = part * jnp.concatenate([lax.rsqrt(pivots)] * repeat, axis=1)
        inverse[first:last, :] = jnp.where(lane < last, part, 0.0)
        if last < n:
            rest = work[last:, :]
            lane_rest = lax.broadcasted_iota(jnp.int32, rest.shape, 1)
            rest = jnp.where((lane_rest >= first) & (lane_rest < last), 0.0, rest)
            work[last:, :] = rest - lax.dot_general(
                part[:, last:],
                part,
                (((0,), (0,)), ((), ())),
                precision=lax.Precision.HIGHEST,
                preferred_element_type=jnp.float32,
            )


def inverse_factor(gram):
    n = gram.shape[0]
    return pl.pallas_call(
        factor_kernel,
        out_shape=jax.ShapeDtypeStruct((n, n), jnp.float32),
        scratch_shapes=[pltpu.VMEM((n, n), jnp.float32)],
        cost_estimate=pl.CostEstimate(flops=10**10, bytes_accessed=8 * n * n, transcendentals=0),
        name="inverse_factor",
    )(gram)


def back_kernel(inverse, s0, s1, s2, s3, s4, s5, s6, s7, back, norms):
    row = lax.axis_index("row")
    for n, share in enumerate((s0, s1, s2, s3, s4, s5, s6, s7)):
        height = share.shape[0]
        shift = (n + 1) // 2 if n % 2 == 0 else ROWS - (n + 1) // 2
        start = pl.multiple_of(lax.rem(row + shift, ROWS) * height, height)
        back[pl.ds(start, height), :] = dot3(share[...], inverse[...], ((1,), (1,)))
    whole = back[...]
    norms[...] = jnp.sum(whole * whole, axis=0, keepdims=True)


def back_and_norms(inverse, shares):
    rank = inverse.shape[0]
    cols = len(shares) * shares[0].shape[0]
    return call(back_kernel, "back_and_norms", [(cols, rank), (1, rank)], inverse, *shares)


def momentum_kernel(buffer, ortho, back, new_momentum):
    fix = lax.dot_general(
        ortho[...].astype(jnp.bfloat16),
        back[...].astype(jnp.bfloat16),
        (((1,), (1,)), ((), ())),
        preferred_element_type=jnp.float32,
    )
    new_momentum[...] = buffer[...] - (1.0 - keep_rate) * fix


def update_momentum(buffer, ortho, back):
    rows, cols = buffer.shape
    rank = ortho.shape[1]
    tile = rows // TILES
    part = lambda width: pl.BlockSpec((tile, width), lambda i: (i, 0))
    return pl.pallas_call(
        momentum_kernel,
        grid=(TILES,),
        in_specs=[part(cols), part(rank), pl.BlockSpec(back.shape, lambda i: (0, 0))],
        out_specs=part(cols),
        out_shape=jax.ShapeDtypeStruct((rows, cols), jnp.float32),
        compiler_params=pltpu.CompilerParams(vmem_limit_bytes=VMEM_LIMIT),
        name="update_momentum",
    )(buffer, ortho, back)


def weight_kernel(weight, ortho, back, scale, new_weight, new_basis, basis, stepped, sems):
    factor = step_rate * math.sqrt(D * FF / RANK)
    right = back[...]
    basis[...] = right * scale[...]
    stores = []

    def store(source, target):
        copy = pltpu.make_async_copy(source, target, sems.at[len(stores)])
        copy.start()
        stores.append(copy)

    store(basis, new_basis)
    tile = weight.shape[0] // TILES
    for n in range(TILES):
        span = slice(n * tile, (n + 1) * tile)
        step = dot3(ortho[span, :] * scale[...], right, ((1,), (1,)))
        stepped[span, :] = (weight[span, :].astype(jnp.float32) - factor * step).astype(jnp.bfloat16)
        store(stepped.at[span, :], new_weight.at[span, :])
    for copy in stores:
        copy.wait()


def update_weight(weight, ortho, back, scale):
    rows, cols = weight.shape
    rank = ortho.shape[1]
    return pl.pallas_call(
        weight_kernel,
        in_specs=[in_vmem()] * 4,
        out_specs=[pl.BlockSpec(memory_space=pl.ANY)] * 2,
        out_shape=[
            jax.ShapeDtypeStruct((rows, cols), jnp.bfloat16),
            jax.ShapeDtypeStruct((cols, rank), jnp.float32),
        ],
        scratch_shapes=[
            pltpu.VMEM((cols, rank), jnp.float32),
            pltpu.VMEM((rows, cols), jnp.bfloat16),
            pltpu.SemaphoreType.DMA((1 + TILES,)),
        ],
        compiler_params=pltpu.CompilerParams(vmem_limit_bytes=VMEM_LIMIT),
        name="update_weight",
    )(weight, ortho, back, scale)


def call(kernel, name, shape, *args, scalars=0):
    many = isinstance(shape, list)
    return pl.pallas_call(
        kernel,
        in_specs=[pl.BlockSpec(memory_space=pltpu.SMEM)] * scalars + [in_vmem()] * (len(args) - scalars),
        out_specs=[in_vmem()] * len(shape) if many else in_vmem(),
        out_shape=[jax.ShapeDtypeStruct(x, jnp.float32) for x in shape]
        if many
        else jax.ShapeDtypeStruct(shape, jnp.float32),
        compiler_params=pltpu.CompilerParams(vmem_limit_bytes=VMEM_LIMIT),
        name=name,
    )(*args)


def sum_kernel(shares, copies):
    total = shares[0]
    for n in range(1, shares.shape[0]):
        total = total + shares[n]
    for n in range(copies.shape[0]):
        copies[n] = total


def sum_copies(shares, count):
    return call(sum_kernel, "sum_copies", (count,) + shares.shape[1:], shares)


def pick_kernel(core, part, other, mine):
    cut = mine.shape[0]
    span = pl.ds(pl.multiple_of(core[0] * cut, cut), cut)
    mine[...] = part[span, :] + other[span, :]


def gram_kernel(col, mine, other, copies):
    gram = jnp.zeros((mine.shape[1], mine.shape[1]), jnp.float32)
    for half in (mine, other):
        gram = gram + lax.dot_general(
            half[...],
            half[...],
            (((0,), (0,)), ((), ())),
            precision=lax.Precision.HIGHEST,
            preferred_element_type=jnp.float32,
        )
    copies[0] = jnp.zeros(copies.shape[1:], jnp.float32)
    height = copies.shape[1]
    for n in range(COLS):

        @pl.when(col[0] == n)
        def _():
            for m in range(copies.shape[0]):
                copies[m] = gram[n * height : (n + 1) * height, :]


def part_kernel(local, mixed, small, part):
    high, low = split(small[...])
    rank = small.shape[1]
    both = lax.dot_general(
        mixed[...],
        jnp.concatenate([high, low], axis=1),
        (((0,), (0,)), ((), ())),
        preferred_element_type=jnp.float32,
    )
    part[...] = local[...] + (both[:, :rank] + both[:, rank:])


def proj_part(local, mixed, small):
    return pl.pallas_call(
        part_kernel,
        in_specs=[in_vmem()] * 3,
        out_specs=in_vmem(),
        out_shape=jax.ShapeDtypeStruct(local.shape, jnp.float32),
        compiler_params=pltpu.CompilerParams(vmem_limit_bytes=VMEM_LIMIT),
        name="proj_part",
    )(local, mixed, small)


def on_device(acts, out_grads, weight, momentum, basis):
    high = lax.Precision.HIGH
    highest = lax.Precision.HIGHEST
    row = lax.axis_index("row")
    col = lax.axis_index("col")
    core = (col % 2).reshape(1)
    rank = basis.shape[1]

    with jax.named_scope("gather_acts"):
        acts_all = lax.all_gather(acts, "col", axis=0, tiled=True)

    pieces, places = [out_grads], [row]
    up = down = out_grads

    def turn(step, *others):
        nonlocal up, down
        with jax.named_scope("gather_grads"):
            up = lax.ppermute(up, "row", UP)
            down = lax.ppermute(down, "row", DOWN)
            pieces.extend([up, down])
            places.extend([row - step, row + step])
            up, down, *others = lax.optimization_barrier((up, down, *others))
            return others

    with jax.named_scope("proj"):
        mixed = acts.reshape(ROWS, -1, acts.shape[1])
        mixed = lax.all_to_all(mixed, "col", 0, 0, axis_index_groups=MIXERS)
        small = jnp.dot(out_grads.astype(jnp.float32), basis, precision=high)
        small = small.reshape(GROUPS, ROWS, -1, rank).swapaxes(0, 1).reshape(COLS, -1, rank)
        local = jnp.dot(momentum, basis, precision=high)
        small, mixed, local = turn(1, small, mixed, local)
        small = sum_copies(lax.all_to_all(small, "col", 0, 0), ROWS)
        small, mixed = turn(2, small, mixed)
        small = lax.all_to_all(small, "row", 0, 0).reshape(-1, rank)
        part = proj_part(local, mixed.reshape(-1, acts.shape[1]), small)
        (part,) = turn(3, part)

    with jax.named_scope("gather_grads"):
        pieces.append(lax.ppermute(up, "row", UP))
        places.append(row + ROWS // 2)
        place = jnp.stack(places).astype(jnp.int32) % ROWS

    with jax.named_scope("sum_proj"):
        cut = part.shape[0] // 2
        other = lax.ppermute(part, "col", CORE_SWAP)
        mine = call(pick_kernel, "pick", (cut, rank), core, part, other, scalars=1)
        shares = mine.reshape(CHIPS, cut // CHIPS, rank)
        shares = lax.all_to_all(shares, "col", 0, 0, axis_index_groups=SAME_CORE)
        buffer = add_grad(place, acts_all, pieces, momentum)
        mine = sum_copies(shares, CHIPS)
        mine = lax.all_to_all(mine, "col", 0, 0, axis_index_groups=SAME_CORE).reshape(cut, rank)
        mine, buffer = lax.optimization_barrier((mine, buffer))
        other = lax.ppermute(mine, "col", CORE_SWAP)

    with jax.named_scope("cross"):
        cross = call(cross_kernel, "cross", (buffer.shape[1], rank), core, buffer, mine, other, scalars=1)
        cross, mine, other = lax.optimization_barrier((cross, mine, other))
        share = lax.psum_scatter(cross, "row", scatter_dimension=0, tiled=True)

    with jax.named_scope("gram"):
        height = rank // COLS
        gram = call(gram_kernel, "gram", (ROWS, height, rank), col.reshape(1), mine, other, scalars=1)
        gram = sum_copies(lax.all_to_all(gram, "row", 0, 0), COLS)
        gram = lax.all_to_all(gram, "col", 0, 0).reshape(rank, rank)

    inverse = inverse_factor(gram)
    share, inverse = lax.optimization_barrier((share, inverse))
    first = core[0] == 0
    proj = jnp.concatenate([jnp.where(first, mine, other), jnp.where(first, other, mine)], axis=0)
    ortho = lax.dot_general(proj, inverse, (((1,), (1,)), ((), ())), precision=highest)

    with jax.named_scope("gather_cross"):
        parts = [share]
        up = down = share
        for _ in range(1, ROWS // 2):
            up = lax.ppermute(up, "row", UP)
            down = lax.ppermute(down, "row", DOWN)
            parts += [up, down]
        parts.append(lax.ppermute(up, "row", UP))

    back, norms = back_and_norms(inverse, parts)

    with jax.named_scope("norms"):
        norms = jnp.sum(spread(norms, "col", COLS), axis=0)
        scale = 1.0 / jnp.sqrt(norms + norm_eps)

    new_momentum = update_momentum(buffer, ortho, back)
    new_weight, new_basis = update_weight(weight, ortho, back, scale)
    return (new_weight, new_momentum, new_basis)


def solution(mesh):
    return jax.shard_map(
        on_device,
        mesh=mesh,
        in_specs=(
            P("col", "row"),
            P("row", "col"),
            P("row", "col"),
            P("row", "col"),
            P("col", None),
        ),
        out_specs=(P("row", "col"), P("row", "col"), P("col", None)),
        check_vma=False,
    )
```

```python
import math

import jax
import jax.numpy as jnp
from jax import lax
from jax.experimental import pallas as pl
from jax.experimental.pallas import tpu as pltpu
from jax.sharding import PartitionSpec as P

D = 8192
FF = 28672
RANK = 256

keep_rate = 0.95
step_rate = 0.01
norm_eps = 1e-06

ROWS = 8
COLS = 32
CHIPS = 16
VMEM_LIMIT = 24 * 1024 * 1024
VMEM_MORE = 44 * 1024 * 1024
BLOCK = 64
STEP = 16
TILES = 4

UP = [(i, (i + 1) % ROWS) for i in range(ROWS)]
DOWN = [(i, (i - 1) % ROWS) for i in range(ROWS)]
CORE_SWAP = [(i, i ^ 1) for i in range(COLS)]
SAME_CORE = [[2 * i + k for i in range(CHIPS)] for k in range(2)]
GROUPS = COLS // ROWS
MIXERS = [[GROUPS * i + k for i in range(ROWS)] for k in range(GROUPS)]


def split(x):
    high = x.astype(jnp.bfloat16)
    low = (x - high.astype(jnp.float32)).astype(jnp.bfloat16)
    return high, low


def dot3(a, b, dims):
    a_high, a_low = split(a)
    b_high, b_low = split(b)

    def mul(x, y):
        return lax.dot_general(x, y, (dims, ((), ())), preferred_element_type=jnp.float32)

    return mul(a_high, b_high) + (mul(a_high, b_low) + mul(a_low, b_high))


def spread(x, axis, size, groups=None):
    copies = jnp.broadcast_to(x[None], (size,) + x.shape)
    return lax.all_to_all(copies, axis, 0, 0, axis_index_groups=groups)


def in_vmem():
    return pl.BlockSpec(memory_space=pltpu.VMEM)


def grad_kernel(place, acts, *refs):
    pieces, (momentum, buffer, left, right, total, sems) = refs[:-6], refs[-6:]
    tokens = right.shape[0] // len(pieces)
    rows = total.shape[0]
    tile = rows // TILES
    fetches = []
    for n, g in enumerate(pieces):
        span = pl.ds(pl.multiple_of(place[n] * tokens, tokens), tokens)
        fetches.append(pltpu.make_async_copy(g, right.at[span, :], sems.at[n]))
    spans = [pl.ds(n * tile, tile) for n in range(TILES)]
    lefts = [pltpu.make_async_copy(acts.at[:, at], left.at[n], sems.at[len(pieces) + n]) for n, at in enumerate(spans)]
    olds = [
        pltpu.make_async_copy(momentum.at[at, :], total.at[at, :], sems.at[len(pieces) + TILES + n])
        for n, at in enumerate(spans)
    ]
    news = [
        pltpu.make_async_copy(total.at[at, :], buffer.at[at, :], sems.at[len(pieces) + 2 * TILES + n])
        for n, at in enumerate(spans)
    ]
    lefts[0].start()
    for copy in fetches:
        copy.start()
    olds[0].start()
    for n in range(1, TILES):
        lefts[n].start()
        olds[n].start()
    for copy in fetches:
        copy.wait()
    for n in range(TILES):
        lefts[n].wait()
        grad = lax.dot_general(
            left[n], right[...], (((0,), (0,)), ((), ())), preferred_element_type=jnp.float32
        )
        olds[n].wait()
        total[spans[n], :] += grad
        news[n].start()
    for copy in news:
        copy.wait()


def add_grad(place, acts, pieces, momentum):
    rows, cols = momentum.shape
    tokens = acts.shape[0]
    anywhere = pl.BlockSpec(memory_space=pl.ANY)
    return pl.pallas_call(
        grad_kernel,
        in_specs=[pl.BlockSpec(memory_space=pltpu.SMEM)] + [anywhere] * (len(pieces) + 2),
        out_specs=anywhere,
        out_shape=jax.ShapeDtypeStruct((rows, cols), jnp.float32),
        scratch_shapes=[
            pltpu.VMEM((TILES, tokens, rows // TILES), jnp.bfloat16),
            pltpu.VMEM((tokens, cols), jnp.bfloat16),
            pltpu.VMEM((rows, cols), jnp.float32),
            pltpu.SemaphoreType.DMA((len(pieces) + 3 * TILES,)),
        ],
        compiler_params=pltpu.CompilerParams(vmem_limit_bytes=VMEM_MORE),
        cost_estimate=pl.CostEstimate(
            flops=2 * tokens * rows * cols,
            bytes_accessed=2 * tokens * (rows + cols) + 8 * rows * cols,
            transcendentals=0,
        ),
        name="add_grad",
    )(place, acts, *pieces, momentum)


def cross_kernel(core, buffer, mine, other, cross):
    cut = mine.shape[0]
    here = pl.ds(pl.multiple_of(core[0] * cut, cut), cut)
    there = pl.ds(pl.multiple_of((1 - core[0]) * cut, cut), cut)
    first = ((0,), (0,))
    cross[...] = dot3(buffer[here, :], mine[...], first) + dot3(buffer[there, :], other[...], first)


def factor_kernel(gram, inverse, work):
    n = gram.shape[0]
    lanes = 128
    repeat = n // lanes
    work[...] = gram[...]
    rows = lax.broadcasted_iota(jnp.int32, (BLOCK, lanes), 0)
    row = lax.broadcasted_iota(jnp.int32, (BLOCK, n), 0)
    lane = lax.broadcasted_iota(jnp.int32, (BLOCK, n), 1)
    for first in range(0, n, BLOCK):
        last = first + BLOCK
        part = work[first:last, :]
        pivots = jnp.ones((BLOCK, lanes), jnp.float32)
        for j in range(0, BLOCK, STEP):
            at = first + j
            cols = [jnp.broadcast_to(part[:, at + k : at + k + 1], (BLOCK, lanes)) for k in range(STEP)]
            unit = jnp.where(lane - first == row, 1.0, 0.0)
            part = jnp.where((lane >= at) & (lane < at + STEP), unit, part)
            ratios = []
            for k in range(STEP):
                here = j + k
                pivot = cols[k][here : here + 1, :]
                pivots = jnp.where(rows == here, pivot, pivots)
                ratio = jnp.where(rows > here, cols[k] * (1.0 / pivot), 0.0)
                ratios.append(ratio)
                for m in range(k + 1, STEP):
                    cols[m] = cols[m] - ratio * cols[m][here : here + 1, :]
            for k in range(STEP):
                here = j + k
                part = part - jnp.concatenate([ratios[k]] * repeat, axis=1) * part[here : here + 1, :]
        part = part * jnp.concatenate([lax.rsqrt(pivots)] * repeat, axis=1)
        inverse[first:last, :] = jnp.where(lane < last, part, 0.0)
        if last < n:
            rest = work[last:, :]
            lane_rest = lax.broadcasted_iota(jnp.int32, rest.shape, 1)
            rest = jnp.where((lane_rest >= first) & (lane_rest < last), 0.0, rest)
            work[last:, :] = rest - lax.dot_general(
                part[:, last:],
                part,
                (((0,), (0,)), ((), ())),
                precision=lax.Precision.HIGHEST,
                preferred_element_type=jnp.float32,
            )


def inverse_factor(gram):
    n = gram.shape[0]
    return pl.pallas_call(
        factor_kernel,
        out_shape=jax.ShapeDtypeStruct((n, n), jnp.float32),
        scratch_shapes=[pltpu.VMEM((n, n), jnp.float32)],
        cost_estimate=pl.CostEstimate(flops=10**10, bytes_accessed=8 * n * n, transcendentals=0),
        name="inverse_factor",
    )(gram)


def back_kernel(inverse, s0, s1, s2, s3, s4, s5, s6, s7, back, norms):
    row = lax.axis_index("row")
    for n, share in enumerate((s0, s1, s2, s3, s4, s5, s6, s7)):
        height = share.shape[0]
        shift = (n + 1) // 2 if n % 2 == 0 else ROWS - (n + 1) // 2
        start = pl.multiple_of(lax.rem(row + shift, ROWS) * height, height)
        back[pl.ds(start, height), :] = dot3(share[...], inverse[...], ((1,), (1,)))
    whole = back[...]
    norms[...] = jnp.sum(whole * whole, axis=0, keepdims=True)


def back_and_norms(inverse, shares):
    rank = inverse.shape[0]
    cols = len(shares) * shares[0].shape[0]
    return call(back_kernel, "back_and_norms", [(cols, rank), (1, rank)], inverse, *shares)


def momentum_kernel(buffer, ortho, back, weight, new_momentum, held, moved, sems):
    fetch = pltpu.make_async_copy(weight, held, sems.at[TILES])
    fetch.start()
    right = back[...].astype(jnp.bfloat16)
    tile = buffer.shape[0] // TILES
    stores = []
    for n in range(TILES):
        span = slice(n * tile, (n + 1) * tile)
        fix = lax.dot_general(
            ortho[span, :].astype(jnp.bfloat16),
            right,
            (((1,), (1,)), ((), ())),
            preferred_element_type=jnp.float32,
        )
        moved[span, :] = buffer[span, :] - (1.0 - keep_rate) * fix
        stores.append(pltpu.make_async_copy(moved.at[span, :], new_momentum.at[span, :], sems.at[n]))
        stores[-1].start()
    for copy in stores:
        copy.wait()
    fetch.wait()


def update_momentum(buffer, ortho, back, weight):
    rows, cols = buffer.shape
    anywhere = pl.BlockSpec(memory_space=pl.ANY)
    return pl.pallas_call(
        momentum_kernel,
        in_specs=[in_vmem()] * 3 + [anywhere],
        out_specs=[anywhere, in_vmem()],
        out_shape=[
            jax.ShapeDtypeStruct((rows, cols), jnp.float32),
            jax.ShapeDtypeStruct(weight.shape, weight.dtype),
        ],
        scratch_shapes=[pltpu.VMEM((rows, cols), jnp.float32), pltpu.SemaphoreType.DMA((TILES + 1,))],
        compiler_params=pltpu.CompilerParams(vmem_limit_bytes=VMEM_LIMIT),
        name="update_momentum",
    )(buffer, ortho, back, weight)


def weight_kernel(weight, ortho, back, scale, new_weight, new_basis, basis, stepped, sems):
    factor = step_rate * math.sqrt(D * FF / RANK)
    right = back[...]
    basis[...] = right * scale[...]
    stores = []

    def store(source, target):
        copy = pltpu.make_async_copy(source, target, sems.at[len(stores)])
        copy.start()
        stores.append(copy)

    store(basis, new_basis)
    tile = weight.shape[0] // TILES
    for n in range(TILES):
        span = slice(n * tile, (n + 1) * tile)
        step = dot3(ortho[span, :] * scale[...], right, ((1,), (1,)))
        stepped[span, :] = (weight[span, :].astype(jnp.float32) - factor * step).astype(jnp.bfloat16)
        store(stepped.at[span, :], new_weight.at[span, :])
    for copy in stores:
        copy.wait()


def update_weight(weight, ortho, back, scale):
    rows, cols = weight.shape
    rank = ortho.shape[1]
    return pl.pallas_call(
        weight_kernel,
        in_specs=[in_vmem()] * 4,
        out_specs=[pl.BlockSpec(memory_space=pl.ANY)] * 2,
        out_shape=[
            jax.ShapeDtypeStruct((rows, cols), jnp.bfloat16),
            jax.ShapeDtypeStruct((cols, rank), jnp.float32),
        ],
        scratch_shapes=[
            pltpu.VMEM((cols, rank), jnp.float32),
            pltpu.VMEM((rows, cols), jnp.bfloat16),
            pltpu.SemaphoreType.DMA((1 + TILES,)),
        ],
        compiler_params=pltpu.CompilerParams(vmem_limit_bytes=VMEM_LIMIT),
        name="update_weight",
    )(weight, ortho, back, scale)


def call(kernel, name, shape, *args, scalars=0):
    many = isinstance(shape, list)
    return pl.pallas_call(
        kernel,
        in_specs=[pl.BlockSpec(memory_space=pltpu.SMEM)] * scalars + [in_vmem()] * (len(args) - scalars),
        out_specs=[in_vmem()] * len(shape) if many else in_vmem(),
        out_shape=[jax.ShapeDtypeStruct(x, jnp.float32) for x in shape]
        if many
        else jax.ShapeDtypeStruct(shape, jnp.float32),
        compiler_params=pltpu.CompilerParams(vmem_limit_bytes=VMEM_LIMIT),
        name=name,
    )(*args)


def sum_kernel(shares, copies):
    total = shares[0]
    for n in range(1, shares.shape[0]):
        total = total + shares[n]
    for n in range(copies.shape[0]):
        copies[n] = total


def sum_copies(shares, count):
    return call(sum_kernel, "sum_copies", (count,) + shares.shape[1:], shares)


def pick_kernel(core, part, other, mine):
    cut = mine.shape[0]
    span = pl.ds(pl.multiple_of(core[0] * cut, cut), cut)
    mine[...] = part[span, :] + other[span, :]


def gram_kernel(col, mine, other, copies):
    gram = jnp.zeros((mine.shape[1], mine.shape[1]), jnp.float32)
    for half in (mine, other):
        gram = gram + lax.dot_general(
            half[...],
            half[...],
            (((0,), (0,)), ((), ())),
            precision=lax.Precision.HIGHEST,
            preferred_element_type=jnp.float32,
        )
    copies[0] = jnp.zeros(copies.shape[1:], jnp.float32)
    height = copies.shape[1]
    for n in range(COLS):

        @pl.when(col[0] == n)
        def _():
            for m in range(copies.shape[0]):
                copies[m] = gram[n * height : (n + 1) * height, :]


def part_kernel(local, mixed, small, part):
    high, low = split(small[...])
    rank = small.shape[1]
    both = lax.dot_general(
        mixed[...],
        jnp.concatenate([high, low], axis=1),
        (((0,), (0,)), ((), ())),
        preferred_element_type=jnp.float32,
    )
    part[...] = local[...] + (both[:, :rank] + both[:, rank:])


def proj_part(local, mixed, small):
    return pl.pallas_call(
        part_kernel,
        in_specs=[in_vmem()] * 3,
        out_specs=in_vmem(),
        out_shape=jax.ShapeDtypeStruct(local.shape, jnp.float32),
        compiler_params=pltpu.CompilerParams(vmem_limit_bytes=VMEM_LIMIT),
        name="proj_part",
    )(local, mixed, small)


def on_device(acts, out_grads, weight, momentum, basis):
    high = lax.Precision.HIGH
    highest = lax.Precision.HIGHEST
    row = lax.axis_index("row")
    col = lax.axis_index("col")
    core = (col % 2).reshape(1)
    rank = basis.shape[1]

    with jax.named_scope("gather_acts"):
        acts_all = lax.all_gather(acts, "col", axis=0, tiled=True)

    pieces, places = [out_grads], [row]
    up = down = out_grads

    def turn(step, *others):
        nonlocal up, down
        with jax.named_scope("gather_grads"):
            up = lax.ppermute(up, "row", UP)
            down = lax.ppermute(down, "row", DOWN)
            pieces.extend([up, down])
            places.extend([row - step, row + step])
            up, down, *others = lax.optimization_barrier((up, down, *others))
            return others

    with jax.named_scope("proj"):
        mixed = acts.reshape(ROWS, -1, acts.shape[1])
        mixed = lax.all_to_all(mixed, "col", 0, 0, axis_index_groups=MIXERS)
        small = jnp.dot(out_grads.astype(jnp.float32), basis, precision=high)
        small = small.reshape(GROUPS, ROWS, -1, rank).swapaxes(0, 1).reshape(COLS, -1, rank)
        local = jnp.dot(momentum, basis, precision=high)
        small, mixed, local = turn(1, small, mixed, local)
        small = sum_copies(lax.all_to_all(small, "col", 0, 0), ROWS)
        small, mixed = turn(2, small, mixed)
        small = lax.all_to_all(small, "row", 0, 0).reshape(-1, rank)
        part = proj_part(local, mixed.reshape(-1, acts.shape[1]), small)
        (part,) = turn(3, part)

    with jax.named_scope("gather_grads"):
        pieces.append(lax.ppermute(up, "row", UP))
        places.append(row + ROWS // 2)
        place = jnp.stack(places).astype(jnp.int32) % ROWS

    with jax.named_scope("sum_proj"):
        cut = part.shape[0] // 2
        other = lax.ppermute(part, "col", CORE_SWAP)
        mine = call(pick_kernel, "pick", (cut, rank), core, part, other, scalars=1)
        shares = mine.reshape(CHIPS, cut // CHIPS, rank)
        shares = lax.all_to_all(shares, "col", 0, 0, axis_index_groups=SAME_CORE)
        buffer = add_grad(place, acts_all, pieces, momentum)
        mine = sum_copies(shares, CHIPS)
        mine = lax.all_to_all(mine, "col", 0, 0, axis_index_groups=SAME_CORE).reshape(cut, rank)
        mine, buffer = lax.optimization_barrier((mine, buffer))
        other = lax.ppermute(mine, "col", CORE_SWAP)

    with jax.named_scope("cross"):
        cross = call(cross_kernel, "cross", (buffer.shape[1], rank), core, buffer, mine, other, scalars=1)
        cross, mine, other = lax.optimization_barrier((cross, mine, other))
        share = lax.psum_scatter(cross, "row", scatter_dimension=0, tiled=True)

    with jax.named_scope("gram"):
        height = rank // COLS
        gram = call(gram_kernel, "gram", (ROWS, height, rank), col.reshape(1), mine, other, scalars=1)
        gram = sum_copies(lax.all_to_all(gram, "row", 0, 0), COLS)
        gram = lax.all_to_all(gram, "col", 0, 0).reshape(rank, rank)

    inverse = inverse_factor(gram)
    share, inverse = lax.optimization_barrier((share, inverse))
    first = core[0] == 0
    proj = jnp.concatenate([jnp.where(first, mine, other), jnp.where(first, other, mine)], axis=0)
    ortho = lax.dot_general(proj, inverse, (((1,), (1,)), ((), ())), precision=highest)

    with jax.named_scope("gather_cross"):
        parts = [share]
        up = down = share
        for step in range(1, ROWS // 2):
            up = lax.ppermute(up, "row", UP)
            down = lax.ppermute(down, "row", DOWN)
            if step == 1:
                up, down, ortho = lax.optimization_barrier((up, down, ortho))
            parts += [up, down]
        parts.append(lax.ppermute(up, "row", UP))

    back, norms = back_and_norms(inverse, parts)

    with jax.named_scope("norms"):
        norms = jnp.sum(spread(norms, "col", COLS), axis=0)
        scale = 1.0 / jnp.sqrt(norms + norm_eps)

    new_momentum, weight = update_momentum(buffer, ortho, back, weight)
    new_weight, new_basis = update_weight(weight, ortho, back, scale)
    return (new_weight, new_momentum, new_basis)


def solution(mesh):
    return jax.shard_map(
        on_device,
        mesh=mesh,
        in_specs=(
            P("col", "row"),
            P("row", "col"),
            P("row", "col"),
            P("row", "col"),
            P("col", None),
        ),
        out_specs=(P("row", "col"), P("row", "col"), P("col", None)),
        check_vma=False,
    )
```

```python
import math

import jax
import jax.numpy as jnp
from jax import lax
from jax.experimental import pallas as pl
from jax.experimental.pallas import tpu as pltpu
from jax.sharding import PartitionSpec as P

D = 8192
FF = 28672
RANK = 256

keep_rate = 0.95
step_rate = 0.01
norm_eps = 1e-06

ROWS = 8
COLS = 32
CHIPS = 16
VMEM_LIMIT = 24 * 1024 * 1024
VMEM_MOST = 60 * 1024 * 1024
BLOCK = 64
STEP = 16
TILES = 4

UP = [(i, (i + 1) % ROWS) for i in range(ROWS)]
DOWN = [(i, (i - 1) % ROWS) for i in range(ROWS)]
CORE_SWAP = [(i, i ^ 1) for i in range(COLS)]
SAME_CORE = [[2 * i + k for i in range(CHIPS)] for k in range(2)]
GROUPS = COLS // ROWS
MIXERS = [[GROUPS * i + k for i in range(ROWS)] for k in range(GROUPS)]


def split(x):
    high = x.astype(jnp.bfloat16)
    low = (x - high.astype(jnp.float32)).astype(jnp.bfloat16)
    return high, low


def dot3(a, b, dims):
    a_high, a_low = split(a)
    b_high, b_low = split(b)

    def mul(x, y):
        return lax.dot_general(x, y, (dims, ((), ())), preferred_element_type=jnp.float32)

    return mul(a_high, b_high) + (mul(a_high, b_low) + mul(a_low, b_high))


def in_vmem():
    return pl.BlockSpec(memory_space=pltpu.VMEM)


def shift(n):
    return (n + 1) // 2 if n % 2 == 0 else ROWS - (n + 1) // 2


def grad_kernel(acts, *refs):
    pieces, (momentum, buffer, left, right, total, sems) = refs[:-6], refs[-6:]
    tokens = right.shape[0] // len(pieces)
    rows = total.shape[0]
    tile = rows // TILES
    row = lax.axis_index("row")
    fetches = []
    for n, g in enumerate(pieces):
        span = pl.ds(pl.multiple_of(lax.rem(row + shift(n), ROWS) * tokens, tokens), tokens)
        fetches.append(pltpu.make_async_copy(g, right.at[span, :], sems.at[n]))
    spans = [pl.ds(n * tile, tile) for n in range(TILES)]
    lefts = [pltpu.make_async_copy(acts.at[:, at], left.at[n], sems.at[len(pieces) + n]) for n, at in enumerate(spans)]
    olds = [
        pltpu.make_async_copy(momentum.at[at, :], total.at[at, :], sems.at[len(pieces) + TILES + n])
        for n, at in enumerate(spans)
    ]
    news = [
        pltpu.make_async_copy(total.at[at, :], buffer.at[at, :], sems.at[len(pieces) + 2 * TILES + n])
        for n, at in enumerate(spans)
    ]
    lefts[0].start()
    for copy in fetches:
        copy.start()
    olds[0].start()
    for n in range(1, TILES):
        lefts[n].start()
        olds[n].start()
    for copy in fetches:
        copy.wait()
    for n in range(TILES):
        lefts[n].wait()
        grad = lax.dot_general(
            left[n], right[...], (((0,), (0,)), ((), ())), preferred_element_type=jnp.float32
        )
        olds[n].wait()
        total[spans[n], :] += grad
        news[n].start()
    for copy in news:
        copy.wait()


def add_grad(acts, pieces, momentum):
    rows, cols = momentum.shape
    tokens = acts.shape[0]
    anywhere = pl.BlockSpec(memory_space=pl.ANY)
    return pl.pallas_call(
        grad_kernel,
        in_specs=[anywhere] * (len(pieces) + 2),
        out_specs=anywhere,
        out_shape=jax.ShapeDtypeStruct((rows, cols), jnp.float32),
        scratch_shapes=[
            pltpu.VMEM((TILES, tokens, rows // TILES), jnp.bfloat16),
            pltpu.VMEM((tokens, cols), jnp.bfloat16),
            pltpu.VMEM((rows, cols), jnp.float32),
            pltpu.SemaphoreType.DMA((len(pieces) + 3 * TILES,)),
        ],
        compiler_params=pltpu.CompilerParams(vmem_limit_bytes=VMEM_MOST),
        cost_estimate=pl.CostEstimate(
            flops=2 * tokens * rows * cols,
            bytes_accessed=2 * tokens * (rows + cols) + 8 * rows * cols,
            transcendentals=0,
        ),
        name="add_grad",
    )(acts, *pieces, momentum)


def cross_kernel(core, buffer, mine, other, cross):
    cut = mine.shape[0]
    here = pl.ds(pl.multiple_of(core[0] * cut, cut), cut)
    there = pl.ds(pl.multiple_of((1 - core[0]) * cut, cut), cut)
    first = ((0,), (0,))
    cross[...] = dot3(buffer[here, :], mine[...], first) + dot3(buffer[there, :], other[...], first)


def factor_kernel(gram, inverse, work):
    n = gram.shape[0]
    lanes = 128
    repeat = n // lanes
    work[...] = gram[...]
    rows = lax.broadcasted_iota(jnp.int32, (BLOCK, lanes), 0)
    row = lax.broadcasted_iota(jnp.int32, (BLOCK, n), 0)
    lane = lax.broadcasted_iota(jnp.int32, (BLOCK, n), 1)
    for first in range(0, n, BLOCK):
        last = first + BLOCK
        part = work[first:last, :]
        pivots = jnp.ones((BLOCK, lanes), jnp.float32)
        for j in range(0, BLOCK, STEP):
            at = first + j
            cols = [jnp.broadcast_to(part[:, at + k : at + k + 1], (BLOCK, lanes)) for k in range(STEP)]
            unit = jnp.where(lane - first == row, 1.0, 0.0)
            part = jnp.where((lane >= at) & (lane < at + STEP), unit, part)
            ratios = []
            for k in range(STEP):
                here = j + k
                pivot = cols[k][here : here + 1, :]
                pivots = jnp.where(rows == here, pivot, pivots)
                ratio = jnp.where(rows > here, cols[k] * (1.0 / pivot), 0.0)
                ratios.append(ratio)
                for m in range(k + 1, STEP):
                    cols[m] = cols[m] - ratio * cols[m][here : here + 1, :]
            for k in range(STEP):
                here = j + k
                part = part - jnp.concatenate([ratios[k]] * repeat, axis=1) * part[here : here + 1, :]
        part = part * jnp.concatenate([lax.rsqrt(pivots)] * repeat, axis=1)
        inverse[first:last, :] = jnp.where(lane < last, part, 0.0)
        if last < n:
            rest = work[last:, :]
            lane_rest = lax.broadcasted_iota(jnp.int32, rest.shape, 1)
            rest = jnp.where((lane_rest >= first) & (lane_rest < last), 0.0, rest)
            work[last:, :] = rest - lax.dot_general(
                part[:, last:],
                part,
                (((0,), (0,)), ((), ())),
                precision=lax.Precision.HIGHEST,
                preferred_element_type=jnp.float32,
            )


def inverse_factor(gram):
    n = gram.shape[0]
    return pl.pallas_call(
        factor_kernel,
        out_shape=jax.ShapeDtypeStruct((n, n), jnp.float32),
        scratch_shapes=[pltpu.VMEM((n, n), jnp.float32)],
        cost_estimate=pl.CostEstimate(flops=10**10, bytes_accessed=8 * n * n, transcendentals=0),
        name="inverse_factor",
    )(gram)


def back_kernel(inverse, s0, s1, s2, s3, s4, s5, s6, s7, back, norms):
    row = lax.axis_index("row")
    for n, share in enumerate((s0, s1, s2, s3, s4, s5, s6, s7)):
        height = share.shape[0]
        start = pl.multiple_of(lax.rem(row + shift(n), ROWS) * height, height)
        back[pl.ds(start, height), :] = dot3(share[...], inverse[...], ((1,), (1,)))
    whole = back[...]
    total = jnp.sum(whole * whole, axis=0, keepdims=True)
    for n in range(norms.shape[0]):
        norms[n] = total


def back_and_norms(inverse, shares):
    rank = inverse.shape[0]
    cols = len(shares) * shares[0].shape[0]
    return call(back_kernel, "back_and_norms", [(cols, rank), (COLS, 1, rank)], inverse, *shares)


def momentum_kernel(buffer, ortho, back, new_momentum):
    fix = lax.dot_general(
        ortho[...].astype(jnp.bfloat16),
        back[...].astype(jnp.bfloat16),
        (((1,), (1,)), ((), ())),
        preferred_element_type=jnp.float32,
    )
    new_momentum[...] = buffer[...] - (1.0 - keep_rate) * fix


def update_momentum(buffer, ortho, back):
    rows, cols = buffer.shape
    rank = ortho.shape[1]
    tile = rows // TILES
    part = lambda width: pl.BlockSpec((tile, width), lambda i: (i, 0))
    return pl.pallas_call(
        momentum_kernel,
        grid=(TILES,),
        in_specs=[part(cols), part(rank), pl.BlockSpec(back.shape, lambda i: (0, 0))],
        out_specs=part(cols),
        out_shape=jax.ShapeDtypeStruct((rows, cols), jnp.float32),
        compiler_params=pltpu.CompilerParams(vmem_limit_bytes=VMEM_LIMIT),
        name="update_momentum",
    )(buffer, ortho, back)


def weight_kernel(weight, ortho, back, scale, new_weight, new_basis, basis, stepped, sems):
    factor = step_rate * math.sqrt(D * FF / RANK)
    right = back[...]
    basis[...] = right * scale[...]
    stores = []

    def store(source, target):
        copy = pltpu.make_async_copy(source, target, sems.at[len(stores)])
        copy.start()
        stores.append(copy)

    store(basis, new_basis)
    tile = weight.shape[0] // TILES
    for n in range(TILES):
        span = slice(n * tile, (n + 1) * tile)
        step = dot3(ortho[span, :] * scale[...], right, ((1,), (1,)))
        stepped[span, :] = (weight[span, :].astype(jnp.float32) - factor * step).astype(jnp.bfloat16)
        store(stepped.at[span, :], new_weight.at[span, :])
    for copy in stores:
        copy.wait()


def update_weight(weight, ortho, back, scale):
    rows, cols = weight.shape
    rank = ortho.shape[1]
    return pl.pallas_call(
        weight_kernel,
        in_specs=[in_vmem()] * 4,
        out_specs=[pl.BlockSpec(memory_space=pl.ANY)] * 2,
        out_shape=[
            jax.ShapeDtypeStruct((rows, cols), jnp.bfloat16),
            jax.ShapeDtypeStruct((cols, rank), jnp.float32),
        ],
        scratch_shapes=[
            pltpu.VMEM((cols, rank), jnp.float32),
            pltpu.VMEM((rows, cols), jnp.bfloat16),
            pltpu.SemaphoreType.DMA((1 + TILES,)),
        ],
        compiler_params=pltpu.CompilerParams(vmem_limit_bytes=VMEM_LIMIT),
        name="update_weight",
    )(weight, ortho, back, scale)


def call(kernel, name, shape, *args, scalars=0):
    many = isinstance(shape, list)
    return pl.pallas_call(
        kernel,
        in_specs=[pl.BlockSpec(memory_space=pltpu.SMEM)] * scalars + [in_vmem()] * (len(args) - scalars),
        out_specs=[in_vmem()] * len(shape) if many else in_vmem(),
        out_shape=[jax.ShapeDtypeStruct(x, jnp.float32) for x in shape]
        if many
        else jax.ShapeDtypeStruct(shape, jnp.float32),
        compiler_params=pltpu.CompilerParams(vmem_limit_bytes=VMEM_LIMIT),
        name=name,
    )(*args)


def sum_kernel(shares, copies):
    total = shares[0]
    for n in range(1, shares.shape[0]):
        total = total + shares[n]
    for n in range(copies.shape[0]):
        copies[n] = total


def sum_copies(shares, count):
    return call(sum_kernel, "sum_copies", (count,) + shares.shape[1:], shares)


def pick_kernel(core, part, other, mine):
    cut = mine.shape[0]
    span = pl.ds(pl.multiple_of(core[0] * cut, cut), cut)
    mine[...] = part[span, :] + other[span, :]


def gram_kernel(col, mine, other, copies):
    gram = jnp.zeros((mine.shape[1], mine.shape[1]), jnp.float32)
    for half in (mine, other):
        gram = gram + lax.dot_general(
            half[...],
            half[...],
            (((0,), (0,)), ((), ())),
            precision=lax.Precision.HIGHEST,
            preferred_element_type=jnp.float32,
        )
    copies[0] = jnp.zeros(copies.shape[1:], jnp.float32)
    height = copies.shape[1]
    for n in range(COLS):

        @pl.when(col[0] == n)
        def _():
            for m in range(copies.shape[0]):
                copies[m] = gram[n * height : (n + 1) * height, :]


def part_kernel(local, mixed, small, part):
    high, low = split(small[...])
    rank = small.shape[1]
    both = lax.dot_general(
        mixed[...],
        jnp.concatenate([high, low], axis=1),
        (((0,), (0,)), ((), ())),
        preferred_element_type=jnp.float32,
    )
    part[...] = local[...] + (both[:, :rank] + both[:, rank:])


def proj_part(local, mixed, small):
    return pl.pallas_call(
        part_kernel,
        in_specs=[in_vmem()] * 3,
        out_specs=in_vmem(),
        out_shape=jax.ShapeDtypeStruct(local.shape, jnp.float32),
        compiler_params=pltpu.CompilerParams(vmem_limit_bytes=VMEM_LIMIT),
        name="proj_part",
    )(local, mixed, small)


def on_device(acts, out_grads, weight, momentum, basis):
    high = lax.Precision.HIGH
    highest = lax.Precision.HIGHEST
    col = lax.axis_index("col")
    core = (col % 2).reshape(1)
    rank = basis.shape[1]

    with jax.named_scope("gather_acts"):
        acts_all = lax.all_gather(acts, "col", axis=0, tiled=True)

    pieces = [out_grads]
    up = down = out_grads

    def turn(*others):
        nonlocal up, down
        with jax.named_scope("gather_grads"):
            up = lax.ppermute(up, "row", UP)
            down = lax.ppermute(down, "row", DOWN)
            pieces.extend([up, down])
            up, down, *others = lax.optimization_barrier((up, down, *others))
            return others

    with jax.named_scope("proj"):
        mixed = acts.reshape(ROWS, -1, acts.shape[1])
        mixed = lax.all_to_all(mixed, "col", 0, 0, axis_index_groups=MIXERS)
        small = jnp.dot(out_grads.astype(jnp.float32), basis, precision=high)
        small = small.reshape(GROUPS, ROWS, -1, rank).swapaxes(0, 1).reshape(COLS, -1, rank)
        local = jnp.dot(momentum, basis, precision=high)
        small, mixed, local = turn(small, mixed, local)
        small = sum_copies(lax.all_to_all(small, "col", 0, 0), ROWS)
        small, mixed = turn(small, mixed)
        small = lax.all_to_all(small, "row", 0, 0).reshape(-1, rank)
        part = proj_part(local, mixed.reshape(-1, acts.shape[1]), small)
        (part,) = turn(part)

    with jax.named_scope("gather_grads"):
        pieces.append(lax.ppermute(up, "row", UP))

    with jax.named_scope("sum_proj"):
        cut = part.shape[0] // 2
        other = lax.ppermute(part, "col", CORE_SWAP)
        mine = call(pick_kernel, "pick", (cut, rank), core, part, other, scalars=1)
        shares = mine.reshape(CHIPS, cut // CHIPS, rank)
        shares = lax.all_to_all(shares, "col", 0, 0, axis_index_groups=SAME_CORE)
        buffer = add_grad(acts_all, pieces, momentum)
        mine = sum_copies(shares, CHIPS)
        mine = lax.all_to_all(mine, "col", 0, 0, axis_index_groups=SAME_CORE).reshape(cut, rank)
        mine, buffer = lax.optimization_barrier((mine, buffer))
        other = lax.ppermute(mine, "col", CORE_SWAP)

    with jax.named_scope("cross"):
        cross = call(cross_kernel, "cross", (buffer.shape[1], rank), core, buffer, mine, other, scalars=1)
        cross, mine, other = lax.optimization_barrier((cross, mine, other))
        share = lax.psum_scatter(cross, "row", scatter_dimension=0, tiled=True)

    with jax.named_scope("gram"):
        height = rank // COLS
        gram = call(gram_kernel, "gram", (ROWS, height, rank), col.reshape(1), mine, other, scalars=1)
        gram = sum_copies(lax.all_to_all(gram, "row", 0, 0), COLS)
        gram = lax.all_to_all(gram, "col", 0, 0).reshape(rank, rank)

    inverse = inverse_factor(gram)
    share, inverse = lax.optimization_barrier((share, inverse))
    first = core[0] == 0
    proj = jnp.concatenate([jnp.where(first, mine, other), jnp.where(first, other, mine)], axis=0)
    ortho = lax.dot_general(proj, inverse, (((1,), (1,)), ((), ())), precision=highest)

    with jax.named_scope("gather_cross"):
        parts = [share]
        up = down = share
        for step in range(1, ROWS // 2):
            up = lax.ppermute(up, "row", UP)
            down = lax.ppermute(down, "row", DOWN)
            if step == 1:
                up, down, ortho = lax.optimization_barrier((up, down, ortho))
            parts += [up, down]
        parts.append(lax.ppermute(up, "row", UP))

    back, norms = back_and_norms(inverse, parts)

    with jax.named_scope("norms"):
        norms = jnp.sum(lax.all_to_all(norms, "col", 0, 0), axis=0)
        scale = 1.0 / jnp.sqrt(norms + norm_eps)

    new_momentum = update_momentum(buffer, ortho, back)
    new_weight, new_basis = update_weight(weight, ortho, back, scale)
    return (new_weight, new_momentum, new_basis)


def solution(mesh):
    return jax.shard_map(
        on_device,
        mesh=mesh,
        in_specs=(
            P("col", "row"),
            P("row", "col"),
            P("row", "col"),
            P("row", "col"),
            P("col", None),
        ),
        out_specs=(P("row", "col"), P("row", "col"), P("col", None)),
        check_vma=False,
    )
```

```python
import math

import jax
import jax.numpy as jnp
from jax import lax
from jax.experimental import pallas as pl
from jax.experimental.pallas import tpu as pltpu
from jax.sharding import PartitionSpec as P

D = 8192
FF = 28672
RANK = 256

keep_rate = 0.95
step_rate = 0.01
norm_eps = 1e-06

ROWS = 8
COLS = 32
CHIPS = 16
VMEM_LIMIT = 24 * 1024 * 1024
VMEM_MOST = 60 * 1024 * 1024
BLOCK = 64
STEP = 16
TILES = 4

UP = [(i, (i + 1) % ROWS) for i in range(ROWS)]
DOWN = [(i, (i - 1) % ROWS) for i in range(ROWS)]
CORE_SWAP = [(i, i ^ 1) for i in range(COLS)]
SAME_CORE = [[2 * i + k for i in range(CHIPS)] for k in range(2)]
GROUPS = COLS // ROWS
MIXERS = [[GROUPS * i + k for i in range(ROWS)] for k in range(GROUPS)]


def split(x):
    high = x.astype(jnp.bfloat16)
    low = (x - high.astype(jnp.float32)).astype(jnp.bfloat16)
    return high, low


def dot3(a, b, dims):
    a_high, a_low = split(a)
    b_high, b_low = split(b)

    def mul(x, y):
        return lax.dot_general(x, y, (dims, ((), ())), preferred_element_type=jnp.float32)

    return mul(a_high, b_high) + (mul(a_high, b_low) + mul(a_low, b_high))


def in_vmem():
    return pl.BlockSpec(memory_space=pltpu.VMEM)


def shift(n):
    return (n + 1) // 2 if n % 2 == 0 else ROWS - (n + 1) // 2


def grad_kernel(acts, *refs):
    pieces, (momentum, buffer, left, right, total, sems) = refs[:-6], refs[-6:]
    tokens = right.shape[0] // len(pieces)
    rows = total.shape[0]
    tile = rows // TILES
    row = lax.axis_index("row")
    fetches = []
    for n, g in enumerate(pieces):
        span = pl.ds(pl.multiple_of(lax.rem(row + shift(n), ROWS) * tokens, tokens), tokens)
        fetches.append(pltpu.make_async_copy(g, right.at[span, :], sems.at[n]))
    spans = [pl.ds(n * tile, tile) for n in range(TILES)]
    lefts = [pltpu.make_async_copy(acts.at[:, at], left.at[n], sems.at[len(pieces) + n]) for n, at in enumerate(spans)]
    olds = [
        pltpu.make_async_copy(momentum.at[at, :], total.at[at, :], sems.at[len(pieces) + TILES + n])
        for n, at in enumerate(spans)
    ]
    news = [
        pltpu.make_async_copy(total.at[at, :], buffer.at[at, :], sems.at[len(pieces) + 2 * TILES + n])
        for n, at in enumerate(spans)
    ]
    lefts[0].start()
    for copy in fetches:
        copy.start()
    olds[0].start()
    for n in range(1, TILES):
        lefts[n].start()
        olds[n].start()
    for copy in fetches:
        copy.wait()
    for n in range(TILES):
        lefts[n].wait()
        grad = lax.dot_general(
            left[n], right[...], (((0,), (0,)), ((), ())), preferred_element_type=jnp.float32
        )
        olds[n].wait()
        total[spans[n], :] += grad
        news[n].start()
    for copy in news:
        copy.wait()


def add_grad(acts, pieces, momentum):
    rows, cols = momentum.shape
    tokens = acts.shape[0]
    anywhere = pl.BlockSpec(memory_space=pl.ANY)
    return pl.pallas_call(
        grad_kernel,
        in_specs=[anywhere] * (len(pieces) + 2),
        out_specs=anywhere,
        out_shape=jax.ShapeDtypeStruct((rows, cols), jnp.float32),
        scratch_shapes=[
            pltpu.VMEM((TILES, tokens, rows // TILES), jnp.bfloat16),
            pltpu.VMEM((tokens, cols), jnp.bfloat16),
            pltpu.VMEM((rows, cols), jnp.float32),
            pltpu.SemaphoreType.DMA((len(pieces) + 3 * TILES,)),
        ],
        compiler_params=pltpu.CompilerParams(vmem_limit_bytes=VMEM_MOST),
        cost_estimate=pl.CostEstimate(
            flops=2 * tokens * rows * cols,
            bytes_accessed=2 * tokens * (rows + cols) + 8 * rows * cols,
            transcendentals=0,
        ),
        name="add_grad",
    )(acts, *pieces, momentum)


def cross_kernel(core, buffer, mine, other, cross):
    cut = mine.shape[0]
    here = pl.ds(pl.multiple_of(core[0] * cut, cut), cut)
    there = pl.ds(pl.multiple_of((1 - core[0]) * cut, cut), cut)
    first = ((0,), (0,))
    cross[...] = dot3(buffer[here, :], mine[...], first) + dot3(buffer[there, :], other[...], first)


def factor_kernel(gram, inverse, work):
    n = gram.shape[0]
    lanes = 128
    repeat = n // lanes
    work[...] = gram[...]
    rows = lax.broadcasted_iota(jnp.int32, (BLOCK, lanes), 0)
    row = lax.broadcasted_iota(jnp.int32, (BLOCK, n), 0)
    lane = lax.broadcasted_iota(jnp.int32, (BLOCK, n), 1)
    for first in range(0, n, BLOCK):
        last = first + BLOCK
        part = work[first:last, :]
        pivots = jnp.ones((BLOCK, lanes), jnp.float32)
        for j in range(0, BLOCK, STEP):
            at = first + j
            cols = [jnp.broadcast_to(part[:, at + k : at + k + 1], (BLOCK, lanes)) for k in range(STEP)]
            unit = jnp.where(lane - first == row, 1.0, 0.0)
            part = jnp.where((lane >= at) & (lane < at + STEP), unit, part)
            ratios = []
            for k in range(STEP):
                here = j + k
                pivot = cols[k][here : here + 1, :]
                pivots = jnp.where(rows == here, pivot, pivots)
                ratio = jnp.where(rows > here, cols[k] * (1.0 / pivot), 0.0)
                ratios.append(ratio)
                for m in range(k + 1, STEP):
                    cols[m] = cols[m] - ratio * cols[m][here : here + 1, :]
            for k in range(STEP):
                here = j + k
                part = part - jnp.concatenate([ratios[k]] * repeat, axis=1) * part[here : here + 1, :]
        part = part * jnp.concatenate([lax.rsqrt(pivots)] * repeat, axis=1)
        inverse[first:last, :] = jnp.where(lane < last, part, 0.0)
        if last < n:
            rest = work[last:, :]
            lane_rest = lax.broadcasted_iota(jnp.int32, rest.shape, 1)
            rest = jnp.where((lane_rest >= first) & (lane_rest < last), 0.0, rest)
            work[last:, :] = rest - lax.dot_general(
                part[:, last:],
                part,
                (((0,), (0,)), ((), ())),
                precision=lax.Precision.HIGHEST,
                preferred_element_type=jnp.float32,
            )


def inverse_factor(gram):
    n = gram.shape[0]
    return pl.pallas_call(
        factor_kernel,
        out_shape=jax.ShapeDtypeStruct((n, n), jnp.float32),
        scratch_shapes=[pltpu.VMEM((n, n), jnp.float32)],
        cost_estimate=pl.CostEstimate(flops=10**10, bytes_accessed=8 * n * n, transcendentals=0),
        name="inverse_factor",
    )(gram)


def back_kernel(inverse, s0, s1, s2, s3, s4, s5, s6, s7, back, norms):
    row = lax.axis_index("row")
    for n, share in enumerate((s0, s1, s2, s3, s4, s5, s6, s7)):
        height = share.shape[0]
        start = pl.multiple_of(lax.rem(row + shift(n), ROWS) * height, height)
        back[pl.ds(start, height), :] = dot3(share[...], inverse[...], ((1,), (1,)))
    whole = back[...]
    total = jnp.sum(whole * whole, axis=0, keepdims=True)
    for n in range(norms.shape[0]):
        norms[n] = total


def back_and_norms(inverse, shares):
    rank = inverse.shape[0]
    cols = len(shares) * shares[0].shape[0]
    return call(back_kernel, "back_and_norms", [(cols, rank), (COLS, 1, rank)], inverse, *shares)


def momentum_kernel(buffer, ortho, back, new_momentum):
    fix = lax.dot_general(
        ortho[...].astype(jnp.bfloat16),
        back[...].astype(jnp.bfloat16),
        (((1,), (1,)), ((), ())),
        preferred_element_type=jnp.float32,
    )
    new_momentum[...] = buffer[...] - (1.0 - keep_rate) * fix


def update_momentum(buffer, ortho, back):
    rows, cols = buffer.shape
    rank = ortho.shape[1]
    tile = rows // TILES
    part = lambda width: pl.BlockSpec((tile, width), lambda i: (i, 0))
    return pl.pallas_call(
        momentum_kernel,
        grid=(TILES,),
        in_specs=[part(cols), part(rank), pl.BlockSpec(back.shape, lambda i: (0, 0))],
        out_specs=part(cols),
        out_shape=jax.ShapeDtypeStruct((rows, cols), jnp.float32),
        compiler_params=pltpu.CompilerParams(vmem_limit_bytes=VMEM_LIMIT),
        name="update_momentum",
    )(buffer, ortho, back)


def weight_kernel(weight, ortho, back, scale, new_weight, new_basis, basis, stepped, sems):
    factor = step_rate * math.sqrt(D * FF / RANK)
    right = back[...]
    basis[...] = right * scale[...]
    stores = []

    def store(source, target):
        copy = pltpu.make_async_copy(source, target, sems.at[len(stores)])
        copy.start()
        stores.append(copy)

    store(basis, new_basis)
    tile = weight.shape[0] // TILES
    for n in range(TILES):
        span = slice(n * tile, (n + 1) * tile)
        step = dot3(ortho[span, :] * scale[...], right, ((1,), (1,)))
        stepped[span, :] = (weight[span, :].astype(jnp.float32) - factor * step).astype(jnp.bfloat16)
        store(stepped.at[span, :], new_weight.at[span, :])
    for copy in stores:
        copy.wait()


def update_weight(weight, ortho, back, scale):
    rows, cols = weight.shape
    rank = ortho.shape[1]
    return pl.pallas_call(
        weight_kernel,
        in_specs=[in_vmem()] * 4,
        out_specs=[pl.BlockSpec(memory_space=pl.ANY)] * 2,
        out_shape=[
            jax.ShapeDtypeStruct((rows, cols), jnp.bfloat16),
            jax.ShapeDtypeStruct((cols, rank), jnp.float32),
        ],
        scratch_shapes=[
            pltpu.VMEM((cols, rank), jnp.float32),
            pltpu.VMEM((rows, cols), jnp.bfloat16),
            pltpu.SemaphoreType.DMA((1 + TILES,)),
        ],
        compiler_params=pltpu.CompilerParams(vmem_limit_bytes=VMEM_LIMIT),
        name="update_weight",
    )(weight, ortho, back, scale)


def call(kernel, name, shape, *args, scalars=0):
    many = isinstance(shape, list)
    return pl.pallas_call(
        kernel,
        in_specs=[pl.BlockSpec(memory_space=pltpu.SMEM)] * scalars + [in_vmem()] * (len(args) - scalars),
        out_specs=[in_vmem()] * len(shape) if many else in_vmem(),
        out_shape=[jax.ShapeDtypeStruct(x, jnp.float32) for x in shape]
        if many
        else jax.ShapeDtypeStruct(shape, jnp.float32),
        compiler_params=pltpu.CompilerParams(vmem_limit_bytes=VMEM_LIMIT),
        name=name,
    )(*args)


def sum_kernel(shares, copies):
    total = shares[0]
    for n in range(1, shares.shape[0]):
        total = total + shares[n]
    for n in range(copies.shape[0]):
        copies[n] = total


def sum_copies(shares, count):
    return call(sum_kernel, "sum_copies", (count,) + shares.shape[1:], shares)


def pick_kernel(core, part, other, mine):
    cut = mine.shape[0]
    span = pl.ds(pl.multiple_of(core[0] * cut, cut), cut)
    mine[...] = part[span, :] + other[span, :]


def gram_kernel(col, mine, other, copies):
    gram = jnp.zeros((mine.shape[1], mine.shape[1]), jnp.float32)
    for half in (mine, other):
        gram = gram + lax.dot_general(
            half[...],
            half[...],
            (((0,), (0,)), ((), ())),
            precision=lax.Precision.HIGHEST,
            preferred_element_type=jnp.float32,
        )
    copies[0] = jnp.zeros(copies.shape[1:], jnp.float32)
    height = copies.shape[1]
    for n in range(COLS):

        @pl.when(col[0] == n)
        def _():
            for m in range(copies.shape[0]):
                copies[m] = gram[n * height : (n + 1) * height, :]


def part_kernel(local, mixed, small, part):
    high, low = split(small[...])
    rank = small.shape[1]
    both = lax.dot_general(
        mixed[...],
        jnp.concatenate([high, low], axis=1),
        (((0,), (0,)), ((), ())),
        preferred_element_type=jnp.float32,
    )
    part[...] = local[...] + (both[:, :rank] + both[:, rank:])


def proj_part(local, mixed, small):
    return pl.pallas_call(
        part_kernel,
        in_specs=[in_vmem()] * 3,
        out_specs=in_vmem(),
        out_shape=jax.ShapeDtypeStruct(local.shape, jnp.float32),
        compiler_params=pltpu.CompilerParams(vmem_limit_bytes=VMEM_LIMIT),
        name="proj_part",
    )(local, mixed, small)


def on_device(acts, out_grads, weight, momentum, basis):
    high = lax.Precision.HIGH
    highest = lax.Precision.HIGHEST
    col = lax.axis_index("col")
    core = (col % 2).reshape(1)
    rank = basis.shape[1]

    with jax.named_scope("gather_acts"):
        acts_all = lax.all_gather(acts, "col", axis=0, tiled=True)

    pieces = [out_grads]
    up = down = out_grads

    def turn(*others):
        nonlocal up, down
        with jax.named_scope("gather_grads"):
            up = lax.ppermute(up, "row", UP)
            down = lax.ppermute(down, "row", DOWN)
            pieces.extend([up, down])
            up, down, *others = lax.optimization_barrier((up, down, *others))
            return others

    with jax.named_scope("proj"):
        mixed = acts.reshape(ROWS, -1, acts.shape[1])
        mixed = lax.all_to_all(mixed, "col", 0, 0, axis_index_groups=MIXERS)
        small = jnp.dot(out_grads.astype(jnp.float32), basis, precision=high)
        small = small.reshape(GROUPS, ROWS, -1, rank).swapaxes(0, 1).reshape(COLS, -1, rank)
        local = jnp.dot(momentum, basis, precision=high)
        small, mixed, local = turn(small, mixed, local)
        small = sum_copies(lax.all_to_all(small, "col", 0, 0), ROWS)
        small, mixed = turn(small, mixed)
        small = lax.all_to_all(small, "row", 0, 0).reshape(-1, rank)
        part = proj_part(local, mixed.reshape(-1, acts.shape[1]), small)
        (part,) = turn(part)

    with jax.named_scope("gather_grads"):
        pieces.append(lax.ppermute(up, "row", UP))

    with jax.named_scope("sum_proj"):
        cut = part.shape[0] // 2
        other = lax.ppermute(part, "col", CORE_SWAP)
        mine = call(pick_kernel, "pick", (cut, rank), core, part, other, scalars=1)
        shares = mine.reshape(CHIPS, cut // CHIPS, rank)
        shares = lax.all_to_all(shares, "col", 0, 0, axis_index_groups=SAME_CORE)
        buffer = add_grad(acts_all, pieces, momentum)
        mine = sum_copies(shares, CHIPS)
        mine = lax.all_to_all(mine, "col", 0, 0, axis_index_groups=SAME_CORE).reshape(cut, rank)
        mine, buffer = lax.optimization_barrier((mine, buffer))
        other = lax.ppermute(mine, "col", CORE_SWAP)

    with jax.named_scope("gram"):
        gram = call(gram_kernel, "gram", (ROWS, rank // COLS, rank), col.reshape(1), mine, other, scalars=1)
        gram, mine, other = lax.optimization_barrier((gram, mine, other))

    with jax.named_scope("cross"):
        cross = call(cross_kernel, "cross", (buffer.shape[1], rank), core, buffer, mine, other, scalars=1)
        cross, gram = lax.optimization_barrier((cross, gram))
        share = lax.psum_scatter(cross, "row", scatter_dimension=0, tiled=True)

    with jax.named_scope("gram"):
        gram = sum_copies(lax.all_to_all(gram, "row", 0, 0), COLS)
        gram = lax.all_to_all(gram, "col", 0, 0).reshape(rank, rank)

    inverse = inverse_factor(gram)
    share, inverse = lax.optimization_barrier((share, inverse))
    first = core[0] == 0
    proj = jnp.concatenate([jnp.where(first, mine, other), jnp.where(first, other, mine)], axis=0)
    ortho = lax.dot_general(proj, inverse, (((1,), (1,)), ((), ())), precision=highest)

    with jax.named_scope("gather_cross"):
        parts = [share]
        up = down = share
        for step in range(1, ROWS // 2):
            up = lax.ppermute(up, "row", UP)
            down = lax.ppermute(down, "row", DOWN)
            if step == 1:
                up, down, ortho = lax.optimization_barrier((up, down, ortho))
            parts += [up, down]
        parts.append(lax.ppermute(up, "row", UP))

    back, norms = back_and_norms(inverse, parts)

    with jax.named_scope("norms"):
        norms = jnp.sum(lax.all_to_all(norms, "col", 0, 0), axis=0)
        scale = 1.0 / jnp.sqrt(norms + norm_eps)

    new_momentum = update_momentum(buffer, ortho, back)
    new_weight, new_basis = update_weight(weight, ortho, back, scale)
    return (new_weight, new_momentum, new_basis)


def solution(mesh):
    return jax.shard_map(
        on_device,
        mesh=mesh,
        in_specs=(
            P("col", "row"),
            P("row", "col"),
            P("row", "col"),
            P("row", "col"),
            P("col", None),
        ),
        out_specs=(P("row", "col"), P("row", "col"), P("col", None)),
        check_vma=False,
    )
```

```python
import math

import jax
import jax.numpy as jnp
from jax import lax
from jax.experimental import pallas as pl
from jax.experimental.pallas import tpu as pltpu
from jax.sharding import PartitionSpec as P

D = 8192
FF = 28672
RANK = 256

keep_rate = 0.95
step_rate = 0.01
norm_eps = 1e-06

ROWS = 8
COLS = 32
CHIPS = 16
VMEM_LIMIT = 24 * 1024 * 1024
VMEM_MOST = 60 * 1024 * 1024
BLOCK = 64
STEP = 16
TILES = 4

UP = [(i, (i + 1) % ROWS) for i in range(ROWS)]
DOWN = [(i, (i - 1) % ROWS) for i in range(ROWS)]
CORE_SWAP = [(i, i ^ 1) for i in range(COLS)]
SAME_CORE = [[2 * i + k for i in range(CHIPS)] for k in range(2)]
GROUPS = COLS // ROWS
MIXERS = [[GROUPS * i + k for i in range(ROWS)] for k in range(GROUPS)]


def split(x):
    high = x.astype(jnp.bfloat16)
    low = (x - high.astype(jnp.float32)).astype(jnp.bfloat16)
    return high, low


def dot3(a, b, dims):
    a_high, a_low = split(a)
    b_high, b_low = split(b)

    def mul(x, y):
        return lax.dot_general(x, y, (dims, ((), ())), preferred_element_type=jnp.float32)

    return mul(a_high, b_high) + (mul(a_high, b_low) + mul(a_low, b_high))


def in_vmem():
    return pl.BlockSpec(memory_space=pltpu.VMEM)


def shift(n):
    return (n + 1) // 2 if n % 2 == 0 else ROWS - (n + 1) // 2


def grad_kernel(acts, *refs):
    pieces, (momentum, buffer, left, right, total, sems) = refs[:-6], refs[-6:]
    tokens = right.shape[0] // len(pieces)
    rows = total.shape[0]
    tile = rows // TILES
    row = lax.axis_index("row")
    fetches = []
    for n, g in enumerate(pieces):
        span = pl.ds(pl.multiple_of(lax.rem(row + shift(n), ROWS) * tokens, tokens), tokens)
        fetches.append(pltpu.make_async_copy(g, right.at[span, :], sems.at[n]))
    spans = [pl.ds(n * tile, tile) for n in range(TILES)]
    lefts = [pltpu.make_async_copy(acts.at[:, at], left.at[n], sems.at[len(pieces) + n]) for n, at in enumerate(spans)]
    olds = [
        pltpu.make_async_copy(momentum.at[at, :], total.at[at, :], sems.at[len(pieces) + TILES + n])
        for n, at in enumerate(spans)
    ]
    news = [
        pltpu.make_async_copy(total.at[at, :], buffer.at[at, :], sems.at[len(pieces) + 2 * TILES + n])
        for n, at in enumerate(spans)
    ]
    lefts[0].start()
    for copy in fetches:
        copy.start()
    olds[0].start()
    for n in range(1, TILES):
        lefts[n].start()
        olds[n].start()
    for copy in fetches:
        copy.wait()
    for n in range(TILES):
        lefts[n].wait()
        grad = lax.dot_general(
            left[n], right[...], (((0,), (0,)), ((), ())), preferred_element_type=jnp.float32
        )
        olds[n].wait()
        total[spans[n], :] += grad
        news[n].start()
    for copy in news:
        copy.wait()


def add_grad(acts, pieces, momentum):
    rows, cols = momentum.shape
    tokens = acts.shape[0]
    anywhere = pl.BlockSpec(memory_space=pl.ANY)
    return pl.pallas_call(
        grad_kernel,
        in_specs=[anywhere] * (len(pieces) + 2),
        out_specs=anywhere,
        out_shape=jax.ShapeDtypeStruct((rows, cols), jnp.float32),
        scratch_shapes=[
            pltpu.VMEM((TILES, tokens, rows // TILES), jnp.bfloat16),
            pltpu.VMEM((tokens, cols), jnp.bfloat16),
            pltpu.VMEM((rows, cols), jnp.float32),
            pltpu.SemaphoreType.DMA((len(pieces) + 3 * TILES,)),
        ],
        compiler_params=pltpu.CompilerParams(vmem_limit_bytes=VMEM_MOST),
        cost_estimate=pl.CostEstimate(
            flops=2 * tokens * rows * cols,
            bytes_accessed=2 * tokens * (rows + cols) + 8 * rows * cols,
            transcendentals=0,
        ),
        name="add_grad",
    )(acts, *pieces, momentum)


def cross_kernel(core, buffer, mine, other, cross):
    cut = mine.shape[0]
    here = pl.ds(pl.multiple_of(core[0] * cut, cut), cut)
    there = pl.ds(pl.multiple_of((1 - core[0]) * cut, cut), cut)
    first = ((0,), (0,))
    cross[...] = dot3(buffer[here, :], mine[...], first) + dot3(buffer[there, :], other[...], first)


def factor_kernel(gram, inverse, work):
    n = gram.shape[0]
    lanes = 128
    repeat = n // lanes
    work[...] = gram[...]
    rows = lax.broadcasted_iota(jnp.int32, (BLOCK, lanes), 0)
    row = lax.broadcasted_iota(jnp.int32, (BLOCK, n), 0)
    lane = lax.broadcasted_iota(jnp.int32, (BLOCK, n), 1)
    for first in range(0, n, BLOCK):
        last = first + BLOCK
        part = work[first:last, :]
        pivots = jnp.ones((BLOCK, lanes), jnp.float32)
        for j in range(0, BLOCK, STEP):
            at = first + j
            cols = [jnp.broadcast_to(part[:, at + k : at + k + 1], (BLOCK, lanes)) for k in range(STEP)]
            unit = jnp.where(lane - first == row, 1.0, 0.0)
            part = jnp.where((lane >= at) & (lane < at + STEP), unit, part)
            ratios = []
            for k in range(STEP):
                here = j + k
                pivot = cols[k][here : here + 1, :]
                pivots = jnp.where(rows == here, pivot, pivots)
                ratio = jnp.where(rows > here, cols[k] * (1.0 / pivot), 0.0)
                ratios.append(ratio)
                for m in range(k + 1, STEP):
                    cols[m] = cols[m] - ratio * cols[m][here : here + 1, :]
            for k in range(STEP):
                here = j + k
                part = part - jnp.concatenate([ratios[k]] * repeat, axis=1) * part[here : here + 1, :]
        part = part * jnp.concatenate([lax.rsqrt(pivots)] * repeat, axis=1)
        inverse[first:last, :] = jnp.where(lane < last, part, 0.0)
        if last < n:
            rest = work[last:, :]
            lane_rest = lax.broadcasted_iota(jnp.int32, rest.shape, 1)
            rest = jnp.where((lane_rest >= first) & (lane_rest < last), 0.0, rest)
            work[last:, :] = rest - lax.dot_general(
                part[:, last:],
                part,
                (((0,), (0,)), ((), ())),
                precision=lax.Precision.HIGHEST,
                preferred_element_type=jnp.float32,
            )


def inverse_factor(gram):
    n = gram.shape[0]
    return pl.pallas_call(
        factor_kernel,
        out_shape=jax.ShapeDtypeStruct((n, n), jnp.float32),
        scratch_shapes=[pltpu.VMEM((n, n), jnp.float32)],
        cost_estimate=pl.CostEstimate(flops=10**10, bytes_accessed=8 * n * n, transcendentals=0),
        name="inverse_factor",
    )(gram)


def early_kernel(inverse, s0, s1, s2, s3, s4, s5, s6, early, sums):
    total = jnp.zeros(sums.shape, jnp.float32)
    for n, share in enumerate((s0, s1, s2, s3, s4, s5, s6)):
        part = dot3(share[...], inverse[...], ((1,), (1,)))
        early[n] = part
        total = total + jnp.sum(part * part, axis=0, keepdims=True)
    sums[...] = total


def late_kernel(inverse, share, early, sums, back, norms):
    row = lax.axis_index("row")
    part = dot3(share[...], inverse[...], ((1,), (1,)))
    height = share.shape[0]
    for n in range(ROWS):
        start = pl.multiple_of(lax.rem(row + shift(n), ROWS) * height, height)
        back[pl.ds(start, height), :] = part if n == ROWS - 1 else early[n]
    total = sums[...] + jnp.sum(part * part, axis=0, keepdims=True)
    for n in range(norms.shape[0]):
        norms[n] = total


def back_and_norms(inverse, shares):
    rank = inverse.shape[0]
    height = shares[0].shape[0]
    early, sums = call(early_kernel, "early", [(ROWS - 1, height, rank), (1, rank)], inverse, *shares[:-1])
    return call(late_kernel, "late", [(ROWS * height, rank), (COLS, 1, rank)], inverse, shares[-1], early, sums)


def momentum_kernel(buffer, ortho, back, new_momentum):
    fix = lax.dot_general(
        ortho[...].astype(jnp.bfloat16),
        back[...].astype(jnp.bfloat16),
        (((1,), (1,)), ((), ())),
        preferred_element_type=jnp.float32,
    )
    new_momentum[...] = buffer[...] - (1.0 - keep_rate) * fix


def update_momentum(buffer, ortho, back):
    rows, cols = buffer.shape
    rank = ortho.shape[1]
    tile = rows // TILES
    part = lambda width: pl.BlockSpec((tile, width), lambda i: (i, 0))
    return pl.pallas_call(
        momentum_kernel,
        grid=(TILES,),
        in_specs=[part(cols), part(rank), pl.BlockSpec(back.shape, lambda i: (0, 0))],
        out_specs=part(cols),
        out_shape=jax.ShapeDtypeStruct((rows, cols), jnp.float32),
        compiler_params=pltpu.CompilerParams(vmem_limit_bytes=VMEM_LIMIT),
        name="update_momentum",
    )(buffer, ortho, back)


def weight_kernel(weight, ortho, back, scale, new_weight, new_basis, basis, stepped, sems):
    factor = step_rate * math.sqrt(D * FF / RANK)
    right = back[...]
    basis[...] = right * scale[...]
    stores = []

    def store(source, target):
        copy = pltpu.make_async_copy(source, target, sems.at[len(stores)])
        copy.start()
        stores.append(copy)

    store(basis, new_basis)
    tile = weight.shape[0] // TILES
    for n in range(TILES):
        span = slice(n * tile, (n + 1) * tile)
        step = dot3(ortho[span, :] * scale[...], right, ((1,), (1,)))
        stepped[span, :] = (weight[span, :].astype(jnp.float32) - factor * step).astype(jnp.bfloat16)
        store(stepped.at[span, :], new_weight.at[span, :])
    for copy in stores:
        copy.wait()


def update_weight(weight, ortho, back, scale):
    rows, cols = weight.shape
    rank = ortho.shape[1]
    return pl.pallas_call(
        weight_kernel,
        in_specs=[in_vmem()] * 4,
        out_specs=[pl.BlockSpec(memory_space=pl.ANY)] * 2,
        out_shape=[
            jax.ShapeDtypeStruct((rows, cols), jnp.bfloat16),
            jax.ShapeDtypeStruct((cols, rank), jnp.float32),
        ],
        scratch_shapes=[
            pltpu.VMEM((cols, rank), jnp.float32),
            pltpu.VMEM((rows, cols), jnp.bfloat16),
            pltpu.SemaphoreType.DMA((1 + TILES,)),
        ],
        compiler_params=pltpu.CompilerParams(vmem_limit_bytes=VMEM_LIMIT),
        name="update_weight",
    )(weight, ortho, back, scale)


def call(kernel, name, shape, *args, scalars=0):
    many = isinstance(shape, list)
    return pl.pallas_call(
        kernel,
        in_specs=[pl.BlockSpec(memory_space=pltpu.SMEM)] * scalars + [in_vmem()] * (len(args) - scalars),
        out_specs=[in_vmem()] * len(shape) if many else in_vmem(),
        out_shape=[jax.ShapeDtypeStruct(x, jnp.float32) for x in shape]
        if many
        else jax.ShapeDtypeStruct(shape, jnp.float32),
        compiler_params=pltpu.CompilerParams(vmem_limit_bytes=VMEM_LIMIT),
        name=name,
    )(*args)


def sum_kernel(shares, copies):
    total = shares[0]
    for n in range(1, shares.shape[0]):
        total = total + shares[n]
    for n in range(copies.shape[0]):
        copies[n] = total


def sum_copies(shares, count):
    return call(sum_kernel, "sum_copies", (count,) + shares.shape[1:], shares)


def pick_kernel(core, part, other, mine):
    cut = mine.shape[0]
    span = pl.ds(pl.multiple_of(core[0] * cut, cut), cut)
    mine[...] = part[span, :] + other[span, :]


def gram_kernel(col, mine, other, copies):
    gram = jnp.zeros((mine.shape[1], mine.shape[1]), jnp.float32)
    for half in (mine, other):
        gram = gram + lax.dot_general(
            half[...],
            half[...],
            (((0,), (0,)), ((), ())),
            precision=lax.Precision.HIGHEST,
            preferred_element_type=jnp.float32,
        )
    copies[0] = jnp.zeros(copies.shape[1:], jnp.float32)
    height = copies.shape[1]
    for n in range(COLS):

        @pl.when(col[0] == n)
        def _():
            for m in range(copies.shape[0]):
                copies[m] = gram[n * height : (n + 1) * height, :]


def part_kernel(local, mixed, small, part):
    high, low = split(small[...])
    rank = small.shape[1]
    both = lax.dot_general(
        mixed[...],
        jnp.concatenate([high, low], axis=1),
        (((0,), (0,)), ((), ())),
        preferred_element_type=jnp.float32,
    )
    part[...] = local[...] + (both[:, :rank] + both[:, rank:])


def proj_part(local, mixed, small):
    return pl.pallas_call(
        part_kernel,
        in_specs=[in_vmem()] * 3,
        out_specs=in_vmem(),
        out_shape=jax.ShapeDtypeStruct(local.shape, jnp.float32),
        compiler_params=pltpu.CompilerParams(vmem_limit_bytes=VMEM_LIMIT),
        name="proj_part",
    )(local, mixed, small)


def on_device(acts, out_grads, weight, momentum, basis):
    high = lax.Precision.HIGH
    highest = lax.Precision.HIGHEST
    col = lax.axis_index("col")
    core = (col % 2).reshape(1)
    rank = basis.shape[1]

    with jax.named_scope("gather_acts"):
        acts_all = lax.all_gather(acts, "col", axis=0, tiled=True)

    pieces = [out_grads]
    up = down = out_grads

    def turn(*others):
        nonlocal up, down
        with jax.named_scope("gather_grads"):
            up = lax.ppermute(up, "row", UP)
            down = lax.ppermute(down, "row", DOWN)
            pieces.extend([up, down])
            up, down, *others = lax.optimization_barrier((up, down, *others))
            return others

    with jax.named_scope("proj"):
        mixed = acts.reshape(ROWS, -1, acts.shape[1])
        mixed = lax.all_to_all(mixed, "col", 0, 0, axis_index_groups=MIXERS)
        small = jnp.dot(out_grads.astype(jnp.float32), basis, precision=high)
        small = small.reshape(GROUPS, ROWS, -1, rank).swapaxes(0, 1).reshape(COLS, -1, rank)
        local = jnp.dot(momentum, basis, precision=high)
        small, mixed, local = turn(small, mixed, local)
        small = sum_copies(lax.all_to_all(small, "col", 0, 0), ROWS)
        small, mixed = turn(small, mixed)
        small = lax.all_to_all(small, "row", 0, 0).reshape(-1, rank)
        part = proj_part(local, mixed.reshape(-1, acts.shape[1]), small)
        (part,) = turn(part)

    with jax.named_scope("gather_grads"):
        pieces.append(lax.ppermute(up, "row", UP))

    with jax.named_scope("sum_proj"):
        cut = part.shape[0] // 2
        other = lax.ppermute(part, "col", CORE_SWAP)
        mine = call(pick_kernel, "pick", (cut, rank), core, part, other, scalars=1)
        shares = mine.reshape(CHIPS, cut // CHIPS, rank)
        shares = lax.all_to_all(shares, "col", 0, 0, axis_index_groups=SAME_CORE)
        buffer = add_grad(acts_all, pieces, momentum)
        mine = sum_copies(shares, CHIPS)
        mine = lax.all_to_all(mine, "col", 0, 0, axis_index_groups=SAME_CORE).reshape(cut, rank)
        mine, buffer = lax.optimization_barrier((mine, buffer))
        other = lax.ppermute(mine, "col", CORE_SWAP)

    with jax.named_scope("gram"):
        gram = call(gram_kernel, "gram", (ROWS, rank // COLS, rank), col.reshape(1), mine, other, scalars=1)
        gram, mine, other = lax.optimization_barrier((gram, mine, other))

    with jax.named_scope("cross"):
        cross = call(cross_kernel, "cross", (buffer.shape[1], rank), core, buffer, mine, other, scalars=1)
        cross, gram = lax.optimization_barrier((cross, gram))
        share = lax.psum_scatter(cross, "row", scatter_dimension=0, tiled=True)

    with jax.named_scope("gram"):
        gram = sum_copies(lax.all_to_all(gram, "row", 0, 0), COLS)
        gram = lax.all_to_all(gram, "col", 0, 0).reshape(rank, rank)

    inverse = inverse_factor(gram)
    share, inverse = lax.optimization_barrier((share, inverse))
    first = core[0] == 0
    proj = jnp.concatenate([jnp.where(first, mine, other), jnp.where(first, other, mine)], axis=0)
    ortho = lax.dot_general(proj, inverse, (((1,), (1,)), ((), ())), precision=highest)

    with jax.named_scope("gather_cross"):
        parts = [share]
        up = down = share
        for step in range(1, ROWS // 2):
            up = lax.ppermute(up, "row", UP)
            down = lax.ppermute(down, "row", DOWN)
            if step == 1:
                up, down, ortho = lax.optimization_barrier((up, down, ortho))
            parts += [up, down]
        parts.append(lax.ppermute(up, "row", UP))

    back, norms = back_and_norms(inverse, parts)

    with jax.named_scope("norms"):
        norms = jnp.sum(lax.all_to_all(norms, "col", 0, 0), axis=0)
        scale = 1.0 / jnp.sqrt(norms + norm_eps)

    new_momentum = update_momentum(buffer, ortho, back)
    new_weight, new_basis = update_weight(weight, ortho, back, scale)
    return (new_weight, new_momentum, new_basis)


def solution(mesh):
    return jax.shard_map(
        on_device,
        mesh=mesh,
        in_specs=(
            P("col", "row"),
            P("row", "col"),
            P("row", "col"),
            P("row", "col"),
            P("col", None),
        ),
        out_specs=(P("row", "col"), P("row", "col"), P("col", None)),
        check_vma=False,
    )
```
